512 devices in a mesh: section: 8 (over y), dp: 32 (over z_lo, x, core), tensor: 2 (over z_hi).
Axes of the slice: x: 4, y: 8, z: 8 (z_hi: 2, z_lo: 4; z = z_hi * 4 + z_lo), core: 2. Of those that a mesh axis runs over, the one named last changes fastest.
Arguments:
- context: bfloat16 [16384, 6144], P('dp', 'section'), may hold values from -64 to 64
- out_weight: bfloat16 [6144, 6144], P('section', ('tensor', 'dp')), may hold values from -0.078125 to 0.078125
- previous: bfloat16 [16384, 6144], P('dp', ('tensor', 'section')), may hold values from -64 to 64
- section_act: bfloat16 [8, 6144, 6144], P('section', 'dp', 'tensor'), may hold values from -6 to 6
- fresh_batch: bfloat16 [6144, 6144], P('dp', 'tensor'), may hold values from -6 to 6
- section_gains: float32 [8, 6144], P('section', 'tensor'), may hold values from 0.1 to 1.9
- mask_blocks: int32 [32, 12], P('dp'), may hold values from 0 to 15, all different within a row
Outputs:
- targets: bfloat16 [16384, 6144], P('dp', ('tensor', 'section'))
- section_out: bfloat16 [8, 6144, 6144], P('section', 'dp', 'tensor')
- target_error: float32 [6144, 6144], P('dp', ('tensor', 'section'))
The draws below stay inside these ranges and needn't reach their ends.
Inputs may be any that keep to these rules, and one draw needn't show every extreme that they name: `mask_blocks`: each row names 12 different blocks.
All inputs are finite; a program needn't handle non-finite values.
Results may differ from the reference program's by a relative error of at most 0.015.
Values may be sent and summed in bfloat16 or wider, within the bound.
No kernel may reach another device: no remote copies, remote signals or barrier semaphores. Data moves between devices by JAX's collectives and lax.ppermute only.
A program may use at most 64 MiB of HBM per device.

```python
import jax
import jax.numpy as jnp
from jax import lax

D = 6144
IMG_DEV = 2
GRID_SIDE = 16
BLOCK_SIDE = 4
MASKED = 12
PATCHES = 256
BLOCKS = 16
MASK_ROWS = 192
N_SECTION = 8
N_DP = 32


def scaled_field(key, row_count, col_count):
    keys = jax.random.split(key, 3)
    base = jnp.clip(jax.random.normal(keys[0], (row_count, col_count), jnp.float32), -4.0, 4.0)
    row_scale = jnp.exp(jax.random.uniform(keys[1], (row_count, 1), jnp.float32, 0.0, 2.3))
    col_scale = jnp.exp(jax.random.uniform(keys[2], (1, col_count), jnp.float32, -0.5, 0.5))
    return jnp.clip(base * row_scale * col_scale * 0.5, -64.0, 64.0)


def ramped_field(key, shape):
    keys = jax.random.split(key, 2)
    place = jnp.arange(D, dtype=jnp.float32) / D
    base = jnp.clip(jax.random.normal(keys[0], shape, jnp.float32), -4.0, 4.0)
    ramp = 0.5 + place
    rough = jnp.exp(jax.random.uniform(keys[1], (D,), jnp.float32, -0.3, 0.3))
    return jnp.clip(base * ramp * rough, -6.0, 6.0)


def draw_context(key, part):
    return scaled_field(jax.random.fold_in(key, 11), N_DP * IMG_DEV * PATCHES, D).astype(jnp.bfloat16)


def draw_previous(key, part):
    return scaled_field(jax.random.fold_in(key, 23), N_DP * IMG_DEV * PATCHES, D).astype(jnp.bfloat16)


def draw_section_act(key, part):
    return ramped_field(jax.random.fold_in(key, 37), (N_SECTION, N_DP * MASK_ROWS, D)).astype(jnp.bfloat16)


def draw_fresh_batch(key, part):
    return ramped_field(jax.random.fold_in(key, 41), (N_DP * MASK_ROWS, D)).astype(jnp.bfloat16)


def shard_levels(stream_key, shape, pieces, low, high):
    gain, own = 1.0, jax.random.fold_in(stream_key, 6)
    for axis_at, blocks in pieces:
        steps = jnp.exp(jax.random.uniform(jax.random.fold_in(own, axis_at), (blocks,), jnp.float32, low / len(pieces), high / len(pieces)))
        gain = gain * jnp.repeat(steps, shape[axis_at] // blocks).reshape([-1 if axis == axis_at else 1 for axis in range(len(shape))])
    return gain


def different_ones(own_key, rows, amount, top, lift):
    order = jax.random.permutation(jax.random.fold_in(own_key, 1), amount)
    boost = order
    for power in range(3):
        boost = boost * boost // amount
    boost = boost * lift // amount
    lots = jax.random.randint(jax.random.fold_in(own_key, 2), (rows, amount), 0, 4096) + boost
    holders = jax.random.permutation(jax.random.fold_in(own_key, 3), rows)[jnp.arange(amount) % rows]
    lots = jnp.where(jnp.arange(rows)[:, None] == holders[None, :], 1 << 14, lots)
    merit = lots * amount + jnp.arange(amount)
    return lax.top_k(merit.astype(jnp.int32), top)[1].astype(jnp.int32)


def bell_draw(stream_key, extent, scale, limit, cuts=(), held_as=jnp.bfloat16):
    result = jax.random.normal(stream_key, extent, jnp.float32) * scale
    if len(cuts) > 0:
        result = shard_levels(stream_key, extent, cuts, -0.22, 0.18) * result
    return jnp.clip(result, min=-limit, max=limit).astype(held_as)


def setup_inputs(seed: int = 0) -> dict:
    streams_of = jax.random.split(jax.random.key(seed), 8)
    context = draw_context(jax.random.fold_in(streams_of[7], 71), 0)
    out_weight = bell_draw(streams_of[1], (D, D), D ** -0.5, 0.078125, ((0, 8), (1, 64)))
    previous = draw_previous(jax.random.fold_in(streams_of[7], 71), 0)
    section_act = draw_section_act(jax.random.fold_in(streams_of[7], 71), 0)
    fresh_batch = draw_fresh_batch(jax.random.fold_in(streams_of[7], 71), 0)
    section_gains = jnp.clip(1.0 + 0.18 * jax.random.normal(streams_of[5], (N_SECTION, D), jnp.float32), 0.1, 1.9)
    mask_blocks = different_ones(streams_of[6], N_DP, BLOCKS, MASKED, 0)
    return {"context": context, "out_weight": out_weight, "previous": previous, "section_act": section_act, "fresh_batch": fresh_batch, "section_gains": section_gains, "mask_blocks": mask_blocks}


def instance_norm(values, images):
    shaped = values.reshape(images, -1, values.shape[-1])
    center = lax.optimization_barrier(jnp.mean(shaped, axis=1, keepdims=True))
    spread = lax.optimization_barrier(jnp.mean(jnp.square(shaped - center), axis=1, keepdims=True))
    return ((shaped - center) * lax.rsqrt(spread + 1e-05)).reshape(values.shape)

def masked_patches(mask_blocks):
    per_side = GRID_SIDE // BLOCK_SIDE
    within = jnp.arange(BLOCK_SIDE * BLOCK_SIDE, dtype=jnp.int32)
    chosen = mask_blocks[..., None]
    grid_row = chosen // per_side * BLOCK_SIDE + within // BLOCK_SIDE
    grid_col = chosen % per_side * BLOCK_SIDE + within % BLOCK_SIDE
    return (grid_row * GRID_SIDE + grid_col).astype(jnp.int32)

def reference(context, out_weight, previous, section_act, fresh_batch, section_gains, mask_blocks):
    block_rows = D // N_SECTION
    projected = jnp.zeros((context.shape[0], D), jnp.float32)
    for section in range(N_SECTION):
        lower = section * block_rows
        partial_term = jnp.dot(context[:, lower:lower + block_rows], out_weight[lower:lower + block_rows], preferred_element_type=jnp.float32).astype(jnp.bfloat16)
        partial_term = lax.optimization_barrier(partial_term)
        projected = projected + partial_term.astype(jnp.float32)
    images = context.shape[0] // PATCHES
    normed_new = instance_norm(projected, images)
    normed_old = instance_norm(previous.astype(jnp.float32), images)
    targets = (0.5 * (normed_new + normed_old)).astype(jnp.bfloat16)
    incoming = jnp.concatenate([fresh_batch[None], section_act[:-1]], axis=0).astype(jnp.float32)
    meansq = lax.optimization_barrier(jnp.mean(incoming * incoming, axis=-1, keepdims=True))
    section_out = (incoming * lax.rsqrt(meansq + 1e-06) * section_gains[:, None, :].astype(jnp.float32)).astype(jnp.bfloat16)
    patch_ids = masked_patches(mask_blocks).reshape(N_DP, MASK_ROWS)
    offsets = (jnp.arange(N_DP, dtype=jnp.int32) * (IMG_DEV * PATCHES)).astype(jnp.int32)
    token_ids = (patch_ids + offsets[:, None]).reshape(-1).astype(jnp.int32)
    picked = jnp.take(targets, token_ids, axis=0).astype(jnp.float32)
    target_error = section_act[N_SECTION - 1].astype(jnp.float32) - picked
    return (targets, section_out, target_error)
```

```python
import jax
import jax.numpy as jnp
from jax import lax
from jax.experimental import pallas as pl
from jax.experimental.pallas import tpu as pltpu
from jax.sharding import Mesh, PartitionSpec as P

GRID_SIDE = 16
BLOCK_SIDE = 4
PATCHES = 256
AXES = ("section", "zlo", "x", "core", "tensor")
DP = ("zlo", "x", "core")


def masked_patches(mask_blocks):
    per_side = GRID_SIDE // BLOCK_SIDE
    within = jnp.arange(BLOCK_SIDE * BLOCK_SIDE, dtype=jnp.int32)
    chosen = mask_blocks[..., None]
    grid_row = chosen // per_side * BLOCK_SIDE + within // BLOCK_SIDE
    grid_col = chosen % per_side * BLOCK_SIDE + within % BLOCK_SIDE
    return grid_row * GRID_SIDE + grid_col


def normed(values, images):
    shaped = values.reshape(images, -1, values.shape[-1])
    center = jnp.mean(shaped, axis=1, keepdims=True)
    off = shaped - center
    spread = jnp.mean(jnp.square(off), axis=1, keepdims=True)
    return (off * lax.rsqrt(spread + 1e-05)).reshape(values.shape)


def product_kernel(context, weight, out):
    rows = weight[...].reshape(-1, weight.shape[-1])
    out[0] = lax.dot_general(
        context[...], rows, (((1,), (1,)), ((), ())), preferred_element_type=jnp.float32
    ).astype(out.dtype)


def products(context, gathered):
    halves, pair, lines, shard, depth = gathered.shape
    rows, count, width = context.shape[0], halves * lines, pair * shard
    return pl.pallas_call(
        product_kernel,
        grid=(count,),
        in_specs=[
            pl.BlockSpec((rows, depth), lambda d: (0, 0)),
            pl.BlockSpec((1, pair, 1, shard, depth), lambda d: (d % 2, 0, d // 2, 0, 0)),
        ],
        out_specs=pl.BlockSpec((1, rows, width), lambda d: (d, 0, 0)),
        out_shape=jax.ShapeDtypeStruct((count, rows, width), jnp.bfloat16),
        compiler_params=pltpu.CompilerParams(vmem_limit_bytes=24 << 20),
        cost_estimate=pl.CostEstimate(
            flops=2 * rows * depth * count * width,
            bytes_accessed=2 * (rows * depth + count * width * (rows + depth)),
            transcendentals=0,
        ),
    )(context, gathered)


def old_kernel(previous, ids, out, hot):
    images = previous.shape[0] // PATCHES
    out[...] = 0.5 * normed(previous[...].astype(jnp.float32), images)
    lane = lax.broadcasted_iota(jnp.int32, hot.shape, 1)
    hot[...] = jnp.where(lane == ids[...], 1.0, 0.0).astype(hot.dtype)


def final_kernel(summed, old, hot, predicted, targets, error):
    images = summed.shape[0] // PATCHES
    new = normed(summed[...].astype(jnp.float32), images)
    made = (0.5 * new + old[...]).astype(targets.dtype)
    targets[...] = made
    picked = jnp.dot(hot[...], made[:PATCHES], preferred_element_type=jnp.float32)
    error[...] = predicted[...].astype(jnp.float32) - picked


def on_device(context, out_weight, previous, section_act, fresh_batch, section_gains, mask_blocks):
    sections = lax.axis_size("section")
    position = lax.axis_index("section")
    rows, width = previous.shape
    act = section_act[0]
    incoming = lax.ppermute(act, "section", [(s, s + 1) for s in range(sections - 1)])
    shards = lax.all_gather(out_weight.T, "zlo", axis=0, tiled=False)
    gathered = lax.all_gather(shards, ("x", "core"), axis=0, tiled=False)
    predicted = lax.dynamic_slice_in_dim(act, (sections - 1) * width, width, 1)
    for s in range(sections - 1):
        piece = lax.ppermute(act[:, s * width:(s + 1) * width], "section", [(sections - 1, s)])
        predicted = jnp.where(position == s, piece, predicted)

    current = jnp.where(position == 0, fresh_batch, incoming)
    wide = current.astype(jnp.float32)
    own = jnp.sum(wide * wide, axis=-1)
    squares = own + lax.ppermute(own, "tensor", [(0, 1), (1, 0)])
    features = act.shape[-1] * lax.axis_size("tensor")
    scaling = lax.rsqrt(squares[:, None] / features + 1e-06)
    section_out = (wide * scaling * section_gains).astype(jnp.bfloat16)[None]

    gathered, section_out, predicted = lax.optimization_barrier((gathered, section_out, predicted))
    gathered = gathered.reshape(2, 4, *shards.shape)
    partial = products(context, gathered)
    summed = lax.psum_scatter(partial, "section", scatter_dimension=0, tiled=False)

    ids = masked_patches(mask_blocks[0]).reshape(-1, 1)
    old, hot = pl.pallas_call(
        old_kernel,
        out_shape=(
            jax.ShapeDtypeStruct((rows, width), jnp.float32),
            jax.ShapeDtypeStruct((ids.shape[0], PATCHES), jnp.bfloat16),
        ),
    )(previous, ids)
    targets, target_error = pl.pallas_call(
        final_kernel,
        out_shape=(
            jax.ShapeDtypeStruct((rows, width), jnp.bfloat16),
            jax.ShapeDtypeStruct((ids.shape[0], width), jnp.float32),
        ),
    )(summed, old, hot, predicted)
    return (targets, section_out, target_error)


def solution(mesh):
    fine = Mesh(mesh.devices.reshape(8, 4, 4, 2, 2), AXES)
    in_specs = (
        P(DP, "section"),
        P("section", ("tensor",) + DP),
        P(DP, ("tensor", "section")),
        P("section", DP, "tensor"),
        P(DP, "tensor"),
        P("section", "tensor"),
        P(DP, None),
    )
    out_specs = (
        P(DP, ("tensor", "section")),
        P("section", DP, "tensor"),
        P(DP, ("tensor", "section")),
    )
    return jax.shard_map(
        on_device, mesh=fine, in_specs=in_specs, out_specs=out_specs, check_vma=False
    )
```

```python
import jax
import jax.numpy as jnp
from jax import lax
from jax.experimental import pallas as pl
from jax.experimental.pallas import tpu as pltpu
from jax.sharding import Mesh, PartitionSpec as P

GRID_SIDE = 16
BLOCK_SIDE = 4
PATCHES = 256
AXES = ("section", "zlo", "x", "core", "tensor")
DP = ("zlo", "x", "core")
FIRST = 40


def masked_patches(mask_blocks):
    per_side = GRID_SIDE // BLOCK_SIDE
    within = jnp.arange(BLOCK_SIDE * BLOCK_SIDE, dtype=jnp.int32)
    chosen = mask_blocks[..., None]
    grid_row = chosen // per_side * BLOCK_SIDE + within // BLOCK_SIDE
    grid_col = chosen % per_side * BLOCK_SIDE + within % BLOCK_SIDE
    return grid_row * GRID_SIDE + grid_col


def normed(values, images):
    shaped = values.reshape(images, -1, values.shape[-1])
    center = jnp.mean(shaped, axis=1, keepdims=True)
    off = shaped - center
    spread = jnp.mean(jnp.square(off), axis=1, keepdims=True)
    return (off * lax.rsqrt(spread + 1e-05)).reshape(values.shape)


def product_kernel(context, mine, other, rest, out):
    pieces = []
    for half in range(2):
        small, large = mine.shape[1] // 2, rest.shape[2] // 2
        pieces.append(mine[0, half * small:(half + 1) * small])
        pieces.append(other[0, half * small:(half + 1) * small])
        pieces.append(rest[0, 0, half * large:(half + 1) * large])
        pieces.append(rest[0, 1, half * large:(half + 1) * large])
    made = lax.dot_general(
        context[...],
        jnp.concatenate(pieces, axis=0),
        (((1,), (1,)), ((), ())),
        preferred_element_type=jnp.float32,
    ).astype(out.dtype)
    width = out.shape[-1]
    out[0] = made[:, :width]
    out[1] = made[:, width:]


def products(context, mine, other, rest):
    rows, depth = context.shape
    lines, small, _ = mine.shape
    large = rest.shape[2]
    width = small + large
    return pl.pallas_call(
        product_kernel,
        grid=(lines,),
        in_specs=[
            pl.BlockSpec((rows, depth), lambda z: (0, 0)),
            pl.BlockSpec((1, small, depth), lambda z: (z, 0, 0)),
            pl.BlockSpec((1, small, depth), lambda z: (z, 0, 0)),
            pl.BlockSpec((1, 2, large, depth), lambda z: (z, 0, 0, 0)),
        ],
        out_specs=pl.BlockSpec((2, rows, width), lambda z: (z, 0, 0)),
        out_shape=jax.ShapeDtypeStruct((2 * lines, rows, width), jnp.bfloat16),
        compiler_params=pltpu.CompilerParams(vmem_limit_bytes=56 << 20),
        cost_estimate=pl.CostEstimate(
            flops=4 * rows * depth * lines * width,
            bytes_accessed=2 * (rows * depth + 2 * lines * width * (rows + depth)),
            transcendentals=0,
        ),
    )(context, mine, other, rest)


def column_order(core, shard):
    pair = jnp.arange(2)[:, None]
    early, late = jnp.arange(FIRST), jnp.arange(FIRST, shard)
    place = lambda held, columns: (pair * 2 * shard + held * shard + columns).reshape(-1)
    return jnp.concatenate(
        [place(core, early), place(1 - core, early), place(0, late), place(1, late)]
    ).astype(jnp.int32)


def ready_kernel(previous, ids, order, out, hot, moved):
    images = previous.shape[0] // PATCHES
    out[...] = 0.5 * normed(previous[...].astype(jnp.float32), images)
    for table, index in ((hot, ids), (moved, order)):
        lane = lax.broadcasted_iota(jnp.int32, table.shape, 1)
        table[...] = jnp.where(lane == index[...], 1.0, 0.0).astype(table.dtype)


def final_kernel(summed, old, hot, moved, predicted, targets, error):
    images = summed.shape[0] // PATCHES
    ordered = jnp.dot(summed[...], moved[...], preferred_element_type=jnp.float32)
    made = (0.5 * normed(ordered, images) + old[...]).astype(targets.dtype)
    targets[...] = made
    picked = jnp.dot(hot[...], made[:PATCHES], preferred_element_type=jnp.float32)
    error[...] = predicted[...].astype(jnp.float32) - picked


def on_device(context, out_weight, previous, section_act, fresh_batch, section_gains, mask_blocks):
    sections = lax.axis_size("section")
    position = lax.axis_index("section")
    rows, width = previous.shape
    act = section_act[0]
    depth, shard = out_weight.shape
    incoming = lax.ppermute(act, "section", [(s, (s + 1) % sections) for s in range(sections)])

    group = lax.all_gather(out_weight.T, "x", axis=0, tiled=False)
    early = group[:, :FIRST].reshape(-1, depth)
    late = group[:, FIRST:].reshape(-1, depth)
    rest = lax.all_gather(late, ("zlo", "core"), axis=0, tiled=False)
    mine = lax.all_gather(early, "zlo", axis=0, tiled=False)
    other = lax.ppermute(mine, "core", [(0, 1), (1, 0)])
    rest, other, incoming = lax.optimization_barrier((rest, other, incoming))
    rest = rest.reshape(-1, 2, *late.shape)
    partial = products(context, mine, other, rest)
    summed = lax.psum_scatter(partial, "section", scatter_dimension=0, tiled=False)

    held = jnp.where(position == 0, incoming, act)
    share = lambda s: lax.dynamic_slice_in_dim(held, s * width, width, 1)
    predicted = share(position)
    for hop in range(1, sections // 2):
        last = sections - 1
        piece = lax.ppermute(
            share(jnp.where(position == 0, hop, last - hop)),
            "section",
            [(0, hop), (last, last - hop)],
        )
        here = (position == hop) | (position == last - hop)
        predicted = jnp.where(here, piece, predicted)

    current = jnp.where(position == 0, fresh_batch, incoming)
    wide = current.astype(jnp.float32)
    own = jnp.sum(wide * wide, axis=-1)
    squares = own + lax.ppermute(own, "tensor", [(0, 1), (1, 0)])
    features = act.shape[-1] * lax.axis_size("tensor")
    scaling = lax.rsqrt(squares[:, None] / features + 1e-06)
    section_out = (wide * scaling * section_gains).astype(jnp.bfloat16)[None]

    ids = masked_patches(mask_blocks[0]).reshape(-1, 1)
    order = column_order(lax.axis_index("core"), shard).reshape(-1, 1)
    old, hot, moved = pl.pallas_call(
        ready_kernel,
        out_shape=(
            jax.ShapeDtypeStruct((rows, width), jnp.float32),
            jax.ShapeDtypeStruct((ids.shape[0], PATCHES), jnp.bfloat16),
            jax.ShapeDtypeStruct((width, width), jnp.bfloat16),
        ),
    )(previous, ids, order)
    targets, target_error = pl.pallas_call(
        final_kernel,
        out_shape=(
            jax.ShapeDtypeStruct((rows, width), jnp.bfloat16),
            jax.ShapeDtypeStruct((ids.shape[0], width), jnp.float32),
        ),
    )(summed, old, hot, moved, predicted)
    return (targets, section_out, target_error)


def solution(mesh):
    fine = Mesh(mesh.devices.reshape(8, 4, 4, 2, 2), AXES)
    in_specs = (
        P(DP, "section"),
        P("section", ("tensor",) + DP),
        P(DP, ("tensor", "section")),
        P("section", DP, "tensor"),
        P(DP, "tensor"),
        P("section", "tensor"),
        P(DP, None),
    )
    out_specs = (
        P(DP, ("tensor", "section")),
        P("section", DP, "tensor"),
        P(DP, ("tensor", "section")),
    )
    return jax.shard_map(
        on_device, mesh=fine, in_specs=in_specs, out_specs=out_specs, check_vma=False
    )
```

```python
import jax
import jax.numpy as jnp
from jax import lax
from jax.experimental import pallas as pl
from jax.experimental.pallas import tpu as pltpu
from jax.sharding import Mesh, PartitionSpec as P

GRID_SIDE = 16
BLOCK_SIDE = 4
PATCHES = 256
AXES = ("section", "zlo", "x", "core", "tensor")
DP = ("zlo", "x", "core")
LATE = 3


def around(value, axis, steps):
    count = lax.axis_size(axis)
    return lax.ppermute(value, axis, [(i, (i + steps) % count) for i in range(count)])


def tied(value, *others):
    return lax.optimization_barrier((value, *others))[0]


def masked_patches(mask_blocks):
    per_side = GRID_SIDE // BLOCK_SIDE
    within = jnp.arange(BLOCK_SIDE * BLOCK_SIDE, dtype=jnp.int32)
    chosen = mask_blocks[..., None]
    grid_row = chosen // per_side * BLOCK_SIDE + within // BLOCK_SIDE
    grid_col = chosen % per_side * BLOCK_SIDE + within % BLOCK_SIDE
    return grid_row * GRID_SIDE + grid_col


def normed(values, images):
    shaped = values.reshape(images, -1, values.shape[-1])
    center = jnp.mean(shaped, axis=1, keepdims=True)
    off = shaped - center
    spread = jnp.mean(jnp.square(off), axis=1, keepdims=True)
    return (off * lax.rsqrt(spread + 1e-05)).reshape(values.shape)


def transpose_kernel(first, second, out):
    rows = first.shape[0]
    out[:, :rows] = first[...].T
    out[:, rows:] = second[...].T


def transposed(first, second):
    rows, depth = first.shape
    return pl.pallas_call(
        transpose_kernel,
        out_shape=jax.ShapeDtypeStruct((depth, 2 * rows), first.dtype),
        compiler_params=pltpu.CompilerParams(vmem_limit_bytes=24 << 20),
    )(first, second)


def ready_kernel(previous, ids, out, hot, same):
    images = previous.shape[0] // PATCHES
    out[...] = 0.5 * normed(previous[...].astype(jnp.float32), images)
    lane = lax.broadcasted_iota(jnp.int32, hot.shape, 1)
    hot[...] = jnp.where(lane == ids[...], 1.0, 0.0).astype(hot.dtype)
    row = lax.broadcasted_iota(jnp.int32, same.shape, 0)
    lane = lax.broadcasted_iota(jnp.int32, same.shape, 1)
    same[...] = jnp.where(lane == row, 1.0, 0.0).astype(same.dtype)


def final_kernel(core, mine, other, old, hot, same, predicted, targets, error):
    images = targets.shape[0] // PATCHES
    shard = mine.shape[0] // 2
    first = core[0] == 0
    pieces = []
    for pair in range(2):
        a, b = (part[pair * shard:(pair + 1) * shard] for part in (mine, other))
        pieces += [jnp.where(first, a, b), jnp.where(first, b, a)]
    ordered = lax.dot_general(
        same[...],
        jnp.concatenate(pieces, axis=0),
        (((1,), (1,)), ((), ())),
        preferred_element_type=jnp.float32,
    )
    made = (0.5 * normed(ordered, images) + old[...]).astype(targets.dtype)
    targets[...] = made
    picked = jnp.dot(hot[...], made[:PATCHES], preferred_element_type=jnp.float32)
    error[...] = predicted[...].astype(jnp.float32) - picked


def on_device(context, out_weight, previous, section_act, fresh_batch, section_gains, mask_blocks):
    f32, bf16 = jnp.float32, jnp.bfloat16
    sections = lax.axis_size("section")
    position, x, core = (lax.axis_index(name) for name in ("section", "x", "core"))
    rows, width = previous.shape
    act = section_act[0]
    depth, shard = out_weight.shape
    far = sections // 2

    held = lax.all_gather(out_weight.T, "zlo", axis=0, tiled=False)
    below = around(held, "x", 1)
    above = around(held, "x", -1)
    incoming = around(act, "section", 1)
    both = transposed(context, around(context, "core", 1))
    opposite = around(below[:LATE], "x", 1)
    opposite_rest = around(above[LATE:], "x", -1)

    def product(weight):
        return jnp.dot(weight, both, preferred_element_type=f32)

    def early_half(dest):
        return (x % 2) ^ (dest % 2 != x // 2).astype(jnp.int32)

    def up(value):
        return around(value.astype(bf16), "section", 1)

    def down(value):
        return around(value.astype(bf16), "section", -1)

    dest = (position + far) % sections
    plane = lambda part: lax.dynamic_index_in_dim(part, dest // 2, 0, keepdims=False)
    near = jnp.where(x % 2 == 0, plane(below), plane(above))
    rising = up(product(jnp.where(dest % 2 == x // 2, plane(held), near)))

    count = lax.axis_size("x")
    weight = jnp.zeros((held.shape[0], count, shard, depth), bf16)
    for part, at, line in (
        (held, x, 0), (below, x + 3, 0), (above, x + 1, 0), (opposite, x + 2, 0), (opposite_rest, x + 2, LATE),
    ):
        weight = lax.dynamic_update_slice(weight, part[:, None], (line, at % count, 0, 0))
    weight = weight.reshape(sections, 2 * shard, depth)

    def block(steps, after=()):
        place = tied(position, *after)
        return lax.dynamic_index_in_dim(weight, (place + steps) % sections, 0, keepdims=False)

    rest = lax.dynamic_slice(weight, (dest, (1 - early_half(dest)) * shard, 0), (1, shard, depth))
    falling = down(product(rest.reshape(shard, depth)))

    def spread(value, half):
        empty = jnp.zeros_like(value)
        return jnp.concatenate([jnp.where(half == 0, value, empty), jnp.where(half == 0, empty, value)])

    half = early_half((position + far - 1) % sections)
    rising = spread(rising, half)
    half = early_half((position + far + 1) % sections)
    falling = spread(falling, 1 - half)
    def round_of(steps, after):
        upward = product(block(steps, after)) + rising.astype(f32)
        downward = product(block(sections - steps, after)) + falling.astype(f32)
        return upward.astype(bf16), downward.astype(bf16)

    sent = round_of(3, ())
    rising, falling = up(sent[0]), down(sent[1])

    ids = masked_patches(mask_blocks[0]).reshape(-1, 1)
    old, hot, same = pl.pallas_call(
        ready_kernel,
        out_shape=(
            jax.ShapeDtypeStruct((rows, width), f32),
            jax.ShapeDtypeStruct((ids.shape[0], PATCHES), bf16),
            jax.ShapeDtypeStruct((rows, rows), bf16),
        ),
        cost_estimate=pl.CostEstimate(flops=0, bytes_accessed=8 << 20, transcendentals=0),
    )(tied(previous, *sent), ids)

    sent = round_of(2, (old,))
    rising, falling = up(sent[0]), down(sent[1])

    last = sections - 1
    source = jnp.where(position == 0, tied(incoming, *sent), act)
    share = lambda s: lax.dynamic_slice_in_dim(source, s * width, width, 1)
    predicted = share(position)
    given = [share(jnp.where(position == 0, hop, last - hop)) for hop in range(1, far)]
    sent = round_of(1, given)
    rising, falling = up(sent[0]), down(sent[1])

    for hop, piece in zip(range(1, far), given):
        piece = lax.ppermute(piece, "section", [(0, hop), (last, last - hop)])
        here = (position == hop) | (position == last - hop)
        predicted = jnp.where(here, piece, predicted)
    current = jnp.where(position == 0, fresh_batch, incoming)
    wide = current.astype(f32)
    own = tied(jnp.sum(wide * wide, axis=-1), *sent)
    squares = own + around(own, "tensor", 1)
    features = act.shape[-1] * lax.axis_size("tensor")
    scaling = lax.rsqrt(squares[:, None] / features + 1e-06)

    summed = (product(block(0, (scaling,))) + rising.astype(f32) + falling.astype(f32)).astype(bf16)
    other = around(summed[:, rows:], "core", 1)
    section_out = (wide * scaling * section_gains).astype(bf16)[None]

    vmem = pl.BlockSpec(memory_space=pltpu.VMEM)
    targets, target_error = pl.pallas_call(
        final_kernel,
        in_specs=[pl.BlockSpec(memory_space=pltpu.SMEM)] + [vmem] * 6,
        out_specs=(vmem, vmem),
        out_shape=(
            jax.ShapeDtypeStruct((rows, width), bf16),
            jax.ShapeDtypeStruct((ids.shape[0], width), f32),
        ),
    )(core.astype(jnp.int32).reshape(1), summed[:, :rows], other, old, hot, same, predicted)
    return (targets, section_out, target_error)


def solution(mesh):
    fine = Mesh(mesh.devices.reshape(8, 4, 4, 2, 2), AXES)
    in_specs = (
        P(DP, "section"),
        P("section", ("tensor",) + DP),
        P(DP, ("tensor", "section")),
        P("section", DP, "tensor"),
        P(DP, "tensor"),
        P("section", "tensor"),
        P(DP, None),
    )
    out_specs = (
        P(DP, ("tensor", "section")),
        P("section", DP, "tensor"),
        P(DP, ("tensor", "section")),
    )
    return jax.shard_map(
        on_device, mesh=fine, in_specs=in_specs, out_specs=out_specs, check_vma=False
    )
```

```python
import jax
import jax.numpy as jnp
from jax import lax
from jax.experimental import pallas as pl
from jax.experimental.pallas import tpu as pltpu
from jax.sharding import Mesh, PartitionSpec as P

GRID_SIDE = 16
BLOCK_SIDE = 4
PATCHES = 256
AXES = ("section", "zlo", "x", "core", "tensor")
DP = ("zlo", "x", "core")


def around(value, axis, steps):
    count = lax.axis_size(axis)
    return lax.ppermute(value, axis, [(i, (i + steps) % count) for i in range(count)])


def tied(value, *others):
    return lax.optimization_barrier((value, *others))[0]


def masked_patches(mask_blocks):
    per_side = GRID_SIDE // BLOCK_SIDE
    within = jnp.arange(BLOCK_SIDE * BLOCK_SIDE, dtype=jnp.int32)
    chosen = mask_blocks[..., None]
    grid_row = chosen // per_side * BLOCK_SIDE + within // BLOCK_SIDE
    grid_col = chosen % per_side * BLOCK_SIDE + within % BLOCK_SIDE
    return grid_row * GRID_SIDE + grid_col


def normed(values, images):
    shaped = values.reshape(images, -1, values.shape[-1])
    center = jnp.mean(shaped, axis=1, keepdims=True)
    off = shaped - center
    spread = jnp.mean(jnp.square(off), axis=1, keepdims=True)
    return (off * lax.rsqrt(spread + 1e-05)).reshape(values.shape)


def transpose_kernel(first, second, out):
    rows = first.shape[0]
    out[:, :rows] = first[...].T
    out[:, rows:] = second[...].T


def transposed(first, second):
    rows, depth = first.shape
    return pl.pallas_call(
        transpose_kernel,
        out_shape=jax.ShapeDtypeStruct((depth, 2 * rows), first.dtype),
    )(first, second)


def ready_kernel(previous, ids, out, hot, same):
    images = previous.shape[0] // PATCHES
    out[...] = 0.5 * normed(previous[...].astype(jnp.float32), images)
    lane = lax.broadcasted_iota(jnp.int32, hot.shape, 1)
    hot[...] = jnp.where(lane == ids[...], 1.0, 0.0).astype(hot.dtype)
    row = lax.broadcasted_iota(jnp.int32, same.shape, 0)
    lane = lax.broadcasted_iota(jnp.int32, same.shape, 1)
    same[...] = jnp.where(lane == row, 1.0, 0.0).astype(same.dtype)


def final_kernel(core, mine, other, old, hot, same, predicted, targets, error):
    images = targets.shape[0] // PATCHES
    shard = mine.shape[0] // 2
    first = core[0] == 0
    pieces = []
    for pair in range(2):
        a, b = (part[pair * shard:(pair + 1) * shard] for part in (mine, other))
        pieces += [jnp.where(first, a, b), jnp.where(first, b, a)]
    ordered = lax.dot_general(
        same[...],
        jnp.concatenate(pieces, axis=0),
        (((1,), (1,)), ((), ())),
        preferred_element_type=jnp.float32,
    )
    made = (0.5 * normed(ordered, images) + old[...]).astype(targets.dtype)
    targets[...] = made
    picked = jnp.dot(hot[...], made[:PATCHES], preferred_element_type=jnp.float32)
    error[...] = predicted[...].astype(jnp.float32) - picked


def on_device(context, out_weight, previous, section_act, fresh_batch, section_gains, mask_blocks):
    f32, bf16 = jnp.float32, jnp.bfloat16
    sections = lax.axis_size("section")
    position, x, core = (lax.axis_index(name) for name in ("section", "x", "core"))
    rows, width = previous.shape
    act = section_act[0]
    depth, shard = out_weight.shape
    far = sections // 2

    held = lax.all_gather(out_weight.T, "zlo", axis=0, tiled=False)
    below = around(held, "x", 1)
    above = around(held, "x", -1)
    incoming = around(act, "section", 1)
    ids = masked_patches(mask_blocks[0]).reshape(-1, 1)
    old, hot, same = pl.pallas_call(
        ready_kernel,
        out_shape=(
            jax.ShapeDtypeStruct((rows, width), f32),
            jax.ShapeDtypeStruct((ids.shape[0], PATCHES), bf16),
            jax.ShapeDtypeStruct((rows, rows), bf16),
        ),
        cost_estimate=pl.CostEstimate(flops=0, bytes_accessed=8 << 20, transcendentals=0),
    )(previous, ids)

    below, incoming, old = lax.optimization_barrier((below, incoming, old))
    opposite = around(below, "x", 1)
    both = transposed(context, around(tied(context, below), "core", 1))

    def product(weight):
        return jnp.dot(weight, both, preferred_element_type=f32)

    def early_half(dest):
        return (x % 2) ^ (dest % 2 != x // 2).astype(jnp.int32)

    def up(value):
        return around(value.astype(bf16), "section", 1)

    def down(value):
        return around(value.astype(bf16), "section", -1)

    dest = (position + far) % sections
    plane = lambda part: lax.dynamic_index_in_dim(part, dest // 2, 0, keepdims=False)
    near = jnp.where(x % 2 == 0, plane(below), plane(above))
    begun = product(jnp.where(dest % 2 == x // 2, plane(held), near)).astype(bf16)
    rising = up(begun)
    last = sections - 1
    cut = lambda value, s, count=1: value[:, s * width:(s + count) * width]
    arrived = tied(incoming, begun)
    given = jnp.where(position == 0, cut(arrived, 2, 2), cut(act, last - 3, 2))
    passed = lax.ppermute(given, "section", [(0, 2), (last, last - 2)])
    opposite = tied(opposite, begun, given)

    count = lax.axis_size("x")
    weight = jnp.zeros((held.shape[0], count, shard, depth), bf16)
    for part, at in (
        (held, x), (below, x + 3), (above, x + 1), (opposite, x + 2),
    ):
        weight = lax.dynamic_update_slice(weight, part[:, None], (0, at % count, 0, 0))
    weight = weight.reshape(sections, 2 * shard, depth)

    def block(steps, after=()):
        place = tied(position, *after)
        return lax.dynamic_index_in_dim(weight, (place + steps) % sections, 0, keepdims=False)

    rest = lax.dynamic_slice(weight, (dest, (1 - early_half(dest)) * shard, 0), (1, shard, depth))
    falling = down(product(rest.reshape(shard, depth)))

    def spread(value, half):
        empty = jnp.zeros_like(value)
        return jnp.concatenate([jnp.where(half == 0, value, empty), jnp.where(half == 0, empty, value)])

    half = early_half((position + far - 1) % sections)
    rising = spread(rising, half)
    half = early_half((position + far + 1) % sections)
    falling = spread(falling, 1 - half)
    def round_of(steps, after):
        upward = product(block(steps, after)) + rising.astype(f32)
        downward = product(block(sections - steps, after)) + falling.astype(f32)
        return upward.astype(bf16), downward.astype(bf16)

    sent = round_of(3, ())
    rising, falling = up(sent[0]), down(sent[1])

    sent = round_of(2, ())
    rising, falling = up(sent[0]), down(sent[1])

    sent = round_of(1, ())
    rising, falling = up(sent[0]), down(sent[1])

    ends = (position == 0) | (position == last)
    low = position < far
    first = position == 0
    onward = jnp.where(first, cut(arrived, 1), jnp.where(ends, cut(act, last - 1), jnp.where(low, cut(passed, 1), cut(passed, 0))))
    handed = lax.ppermute(
        tied(onward, *sent), "section", [(0, 1), (2, 3), (last, last - 1), (last - 2, last - 3)]
    )
    kept = jnp.where(first, cut(arrived, 0), jnp.where(ends, cut(act, last), jnp.where(low, cut(passed, 0), cut(passed, 1))))
    predicted = jnp.where(ends | (position == 2) | (position == last - 2), kept, handed)
    current = jnp.where(position == 0, fresh_batch, incoming)
    wide = current.astype(f32)
    own = tied(jnp.sum(wide * wide, axis=-1), *sent)
    squares = own + around(own, "tensor", 1)
    features = act.shape[-1] * lax.axis_size("tensor")
    scaling = lax.rsqrt(squares[:, None] / features + 1e-06)

    own_term = product(block(0, sent))
    theirs = own_term[:, rows:] + rising[:, rows:].astype(f32) + falling[:, rows:].astype(f32)
    other = around(theirs.astype(bf16), "core", 1)
    section_out = (wide * tied(scaling, theirs) * section_gains).astype(bf16)[None]
    mine = own_term[:, :rows] + rising[:, :rows].astype(f32) + falling[:, :rows].astype(f32)

    vmem = pl.BlockSpec(memory_space=pltpu.VMEM)
    targets, target_error = pl.pallas_call(
        final_kernel,
        in_specs=[pl.BlockSpec(memory_space=pltpu.SMEM)] + [vmem] * 6,
        out_specs=(vmem, vmem),
        out_shape=(
            jax.ShapeDtypeStruct((rows, width), bf16),
            jax.ShapeDtypeStruct(predicted.shape, f32),
        ),
    )(core.astype(jnp.int32).reshape(1), mine.astype(bf16), other, old, hot, same, predicted)
    return (targets, section_out, target_error)


def solution(mesh):
    fine = Mesh(mesh.devices.reshape(8, 4, 4, 2, 2), AXES)
    in_specs = (
        P(DP, "section"),
        P("section", ("tensor",) + DP),
        P(DP, ("tensor", "section")),
        P("section", DP, "tensor"),
        P(DP, "tensor"),
        P("section", "tensor"),
        P(DP, None),
    )
    out_specs = (
        P(DP, ("tensor", "section")),
        P("section", DP, "tensor"),
        P(DP, ("tensor", "section")),
    )
    return jax.shard_map(
        on_device, mesh=fine, in_specs=in_specs, out_specs=out_specs, check_vma=False
    )
```

```python
import jax
import jax.numpy as jnp
from jax import lax
from jax.experimental import pallas as pl
from jax.experimental.pallas import tpu as pltpu
from jax.sharding import Mesh, PartitionSpec as P

GRID_SIDE = 16
BLOCK_SIDE = 4
PATCHES = 256
AXES = ("section", "zlo", "x", "core", "tensor")
DP = ("zlo", "x", "core")


def around(value, axis, steps):
    count = lax.axis_size(axis)
    return lax.ppermute(value, axis, [(i, (i + steps) % count) for i in range(count)])


def tied(value, *others):
    return lax.optimization_barrier((value, *others))[0]


def masked_patches(mask_blocks):
    per_side = GRID_SIDE // BLOCK_SIDE
    within = jnp.arange(BLOCK_SIDE * BLOCK_SIDE, dtype=jnp.int32)
    chosen = mask_blocks[..., None]
    grid_row = chosen // per_side * BLOCK_SIDE + within // BLOCK_SIDE
    grid_col = chosen % per_side * BLOCK_SIDE + within % BLOCK_SIDE
    return grid_row * GRID_SIDE + grid_col


def normed(values, images):
    shaped = values.reshape(images, -1, values.shape[-1])
    center = jnp.mean(shaped, axis=1, keepdims=True)
    off = shaped - center
    spread = jnp.mean(jnp.square(off), axis=1, keepdims=True)
    return (off * lax.rsqrt(spread + 1e-05)).reshape(values.shape)


def transpose_kernel(first, second, out):
    rows = first.shape[0]
    out[:, :rows] = first[...].T
    out[:, rows:] = second[...].T


def transposed(first, second):
    rows, depth = first.shape
    return pl.pallas_call(
        transpose_kernel,
        out_shape=jax.ShapeDtypeStruct((depth, 2 * rows), first.dtype),
    )(first, second)


def product_kernel(x, held, below, above, low, high, context, out):
    plane = pl.program_id(0)
    count = 4
    opposite = jnp.where(plane < count // 2, low[0], high[0])
    weight = jnp.concatenate([held[0], above[0], opposite, below[0]], axis=0)
    made = jnp.dot(weight, context[...], preferred_element_type=jnp.float32).astype(out.dtype)
    shard, rows = held.shape[1], out.shape[-1]
    for steps in range(count):
        at = (x[0] + steps) % count
        for part in range(2):
            out[0, at // 2, part, at % 2] = made[
                steps * shard:(steps + 1) * shard, part * rows:(part + 1) * rows
            ]


def products(x, held, below, above, low, high, context):
    lines, shard, depth = held.shape
    rows = context.shape[1] // 2
    block = lambda index: pl.BlockSpec((1, shard, depth), lambda z: (index(z), 0, 0))
    return pl.pallas_call(
        product_kernel,
        grid=(lines,),
        in_specs=[pl.BlockSpec(memory_space=pltpu.SMEM)]
        + [block(lambda z: z)] * 3
        + [block(lambda z: jnp.minimum(z, lines // 2 - 1)), block(lambda z: jnp.maximum(z - lines // 2, 0))]
        + [pl.BlockSpec(context.shape, lambda z: (0, 0))],
        out_specs=pl.BlockSpec((1, 2, 2, 2, shard, rows), lambda z: (z, 0, 0, 0, 0, 0)),
        out_shape=jax.ShapeDtypeStruct((lines, 2, 2, 2, shard, rows), jnp.bfloat16),
        compiler_params=pltpu.CompilerParams(vmem_limit_bytes=24 << 20),
        cost_estimate=pl.CostEstimate(
            flops=16 * lines * shard * depth * rows,
            bytes_accessed=2 * (8 * lines * shard * rows + 4 * lines * shard * depth + 2 * depth * rows),
            transcendentals=0,
        ),
    )(x, held, below, above, low, high, context)


def ready_kernel(previous, ids, out, hot, same):
    images = previous.shape[0] // PATCHES
    out[...] = 0.5 * normed(previous[...].astype(jnp.float32), images)
    lane = lax.broadcasted_iota(jnp.int32, hot.shape, 1)
    hot[...] = jnp.where(lane == ids[...], 1.0, 0.0).astype(hot.dtype)
    row = lax.broadcasted_iota(jnp.int32, same.shape, 0)
    lane = lax.broadcasted_iota(jnp.int32, same.shape, 1)
    same[...] = jnp.where(lane == row, 1.0, 0.0).astype(same.dtype)


def final_kernel(core, mine, other, old, hot, same, predicted, targets, error):
    images = targets.shape[0] // PATCHES
    shard = mine.shape[0] // 2
    first = core[0] == 0
    pieces = []
    for pair in range(2):
        a, b = (part[pair * shard:(pair + 1) * shard] for part in (mine, other))
        pieces += [jnp.where(first, a, b), jnp.where(first, b, a)]
    ordered = lax.dot_general(
        same[...],
        jnp.concatenate(pieces, axis=0),
        (((1,), (1,)), ((), ())),
        preferred_element_type=jnp.float32,
    )
    made = (0.5 * normed(ordered, images) + old[...]).astype(targets.dtype)
    targets[...] = made
    picked = jnp.dot(hot[...], made[:PATCHES], preferred_element_type=jnp.float32)
    error[...] = predicted[...].astype(jnp.float32) - picked


def on_device(context, out_weight, previous, section_act, fresh_batch, section_gains, mask_blocks):
    f32, bf16 = jnp.float32, jnp.bfloat16
    sections = lax.axis_size("section")
    position, x, core = (lax.axis_index(name) for name in ("section", "x", "core"))
    rows, width = previous.shape
    act = section_act[0]
    depth, shard = out_weight.shape
    far = sections // 2

    held = lax.all_gather(out_weight.T, "zlo", axis=0, tiled=False)
    below = around(held, "x", 1)
    above = around(held, "x", -1)
    incoming = around(act, "section", 1)
    both = transposed(context, around(context, "core", 1))
    below, incoming, both = lax.optimization_barrier((below, incoming, both))
    middle = held.shape[0] // 2
    low = around(below[:middle], "x", 1)
    high = around(above[middle:], "x", -1)
    partial = products(x.astype(jnp.int32).reshape(1), held, below, above, low, high, both)
    partial = partial.reshape(sections, 2, 2 * shard, rows)
    summed = lax.psum_scatter(partial, "section", scatter_dimension=0, tiled=False)
    mine, other = summed[0], around(summed[1], "core", 1)

    last = sections - 1
    first, ends, near = position == 0, (position == 0) | (position == last), position < far
    cut = lambda value, s, count=1: value[:, s * width:(s + count) * width]
    incoming, act, previous = lax.optimization_barrier((incoming, act, previous, partial))[:3]
    passed = lax.ppermute(
        jnp.where(first, cut(incoming, 2, 2), cut(act, last - 3, 2)), "section", [(0, 2), (last, last - 2)]
    )
    onward = jnp.where(
        ends,
        jnp.where(first, cut(incoming, 1), cut(act, last - 1)),
        jnp.where(near, cut(passed, 1), cut(passed, 0)),
    )
    handed = lax.ppermute(onward, "section", [(0, 1), (2, 3), (last, last - 1), (last - 2, last - 3)])
    kept = jnp.where(
        ends,
        jnp.where(first, cut(incoming, 0), cut(act, last)),
        jnp.where(near, cut(passed, 0), cut(passed, 1)),
    )
    predicted = jnp.where(ends | (position == 2) | (position == last - 2), kept, handed)

    current = jnp.where(first, fresh_batch, incoming)
    wide = current.astype(f32)
    own = jnp.sum(wide * wide, axis=-1)
    squares = own + around(own, "tensor", 1)
    features = act.shape[-1] * lax.axis_size("tensor")
    scaling = lax.rsqrt(squares[:, None] / features + 1e-06)
    section_out = (wide * scaling * section_gains).astype(bf16)[None]

    ids = masked_patches(mask_blocks[0]).reshape(-1, 1)
    old, hot, same = pl.pallas_call(
        ready_kernel,
        out_shape=(
            jax.ShapeDtypeStruct((rows, width), f32),
            jax.ShapeDtypeStruct((ids.shape[0], PATCHES), bf16),
            jax.ShapeDtypeStruct((rows, rows), bf16),
        ),
        cost_estimate=pl.CostEstimate(flops=0, bytes_accessed=8 << 20, transcendentals=0),
    )(previous, ids)

    vmem = pl.BlockSpec(memory_space=pltpu.VMEM)
    targets, target_error = pl.pallas_call(
        final_kernel,
        in_specs=[pl.BlockSpec(memory_space=pltpu.SMEM)] + [vmem] * 6,
        out_specs=(vmem, vmem),
        out_shape=(
            jax.ShapeDtypeStruct((rows, width), bf16),
            jax.ShapeDtypeStruct(predicted.shape, f32),
        ),
    )(core.astype(jnp.int32).reshape(1), mine, other, old, hot, same, predicted)
    return (targets, section_out, target_error)


def solution(mesh):
    fine = Mesh(mesh.devices.reshape(8, 4, 4, 2, 2), AXES)
    in_specs = (
        P(DP, "section"),
        P("section", ("tensor",) + DP),
        P(DP, ("tensor", "section")),
        P("section", DP, "tensor"),
        P(DP, "tensor"),
        P("section", "tensor"),
        P(DP, None),
    )
    out_specs = (
        P(DP, ("tensor", "section")),
        P("section", DP, "tensor"),
        P(DP, ("tensor", "section")),
    )
    return jax.shard_map(
        on_device, mesh=fine, in_specs=in_specs, out_specs=out_specs, check_vma=False
    )
```

```python
import jax
import jax.numpy as jnp
from jax import lax
from jax.experimental import pallas as pl
from jax.experimental.pallas import tpu as pltpu
from jax.sharding import Mesh, PartitionSpec as P

GRID_SIDE = 16
BLOCK_SIDE = 4
PATCHES = 256
AXES = ("section", "zlo", "x", "core", "tensor")
DP = ("zlo", "x", "core")
LATE = 3


def around(value, axis, steps):
    count = lax.axis_size(axis)
    return lax.ppermute(value, axis, [(i, (i + steps) % count) for i in range(count)])


def tied(value, *others):
    return lax.optimization_barrier((value, *others))[0]


def masked_patches(mask_blocks):
    per_side = GRID_SIDE // BLOCK_SIDE
    within = jnp.arange(BLOCK_SIDE * BLOCK_SIDE, dtype=jnp.int32)
    chosen = mask_blocks[..., None]
    grid_row = chosen // per_side * BLOCK_SIDE + within // BLOCK_SIDE
    grid_col = chosen % per_side * BLOCK_SIDE + within % BLOCK_SIDE
    return grid_row * GRID_SIDE + grid_col


def normed(values, images):
    shaped = values.reshape(images, -1, values.shape[-1])
    center = jnp.mean(shaped, axis=1, keepdims=True)
    off = shaped - center
    spread = jnp.mean(jnp.square(off), axis=1, keepdims=True)
    return (off * lax.rsqrt(spread + 1e-05)).reshape(values.shape)


def transpose_kernel(first, second, out):
    rows = first.shape[0]
    out[:, :rows] = first[...].T
    out[:, rows:] = second[...].T


def transposed(first, second):
    rows, depth = first.shape
    return pl.pallas_call(
        transpose_kernel,
        out_shape=jax.ShapeDtypeStruct((depth, 2 * rows), first.dtype),
    )(first, second)


def ready_kernel(previous, ids, out, hot, same):
    images = previous.shape[0] // PATCHES
    out[...] = 0.5 * normed(previous[...].astype(jnp.float32), images)
    lane = lax.broadcasted_iota(jnp.int32, hot.shape, 1)
    hot[...] = jnp.where(lane == ids[...], 1.0, 0.0).astype(hot.dtype)
    row = lax.broadcasted_iota(jnp.int32, same.shape, 0)
    lane = lax.broadcasted_iota(jnp.int32, same.shape, 1)
    same[...] = jnp.where(lane == row, 1.0, 0.0).astype(same.dtype)


def final_kernel(place, mine, other, old, hot, same, kept, handed, targets, error):
    images = targets.shape[0] // PATCHES
    shard = mine.shape[0] // 2
    first = place[0] == 0
    pieces = []
    for pair in range(2):
        a, b = (part[pair * shard:(pair + 1) * shard] for part in (mine, other))
        pieces += [jnp.where(first, a, b), jnp.where(first, b, a)]
    ordered = lax.dot_general(
        same[...],
        jnp.concatenate(pieces, axis=0),
        (((1,), (1,)), ((), ())),
        preferred_element_type=jnp.float32,
    )
    made = (0.5 * normed(ordered, images) + old[...]).astype(targets.dtype)
    targets[...] = made
    picked = jnp.dot(hot[...], made[:PATCHES], preferred_element_type=jnp.float32)
    predicted = jnp.where(place[1] == 1, kept[...], handed[...])
    error[...] = predicted.astype(jnp.float32) - picked


def on_device(context, out_weight, previous, section_act, fresh_batch, section_gains, mask_blocks):
    f32, bf16 = jnp.float32, jnp.bfloat16
    sections = lax.axis_size("section")
    position, x, core = (lax.axis_index(name) for name in ("section", "x", "core"))
    rows, width = previous.shape
    act = section_act[0]
    depth, shard = out_weight.shape
    far = sections // 2

    held = lax.all_gather(out_weight.T, "zlo", axis=0, tiled=False)
    below = around(held, "x", 1)
    above = around(held, "x", -1)
    incoming = around(act, "section", 1)
    both = transposed(context, around(context, "core", 1))
    count = lax.axis_size("x")
    weight = jnp.broadcast_to(held[:, None], (held.shape[0], count, shard, depth))

    ids = masked_patches(mask_blocks[0]).reshape(-1, 1)
    old, hot, same = pl.pallas_call(
        ready_kernel,
        out_shape=(
            jax.ShapeDtypeStruct((rows, width), f32),
            jax.ShapeDtypeStruct((ids.shape[0], PATCHES), bf16),
            jax.ShapeDtypeStruct((rows, rows), bf16),
        ),
        cost_estimate=pl.CostEstimate(flops=0, bytes_accessed=8 << 20, transcendentals=0),
    )(previous, ids)

    below, incoming, old, both, weight = lax.optimization_barrier((below, incoming, old, both, weight))
    opposite = around(above[:LATE], "x", -1)
    opposite_rest = around(below[LATE:], "x", 1)

    def product(weight):
        return jnp.dot(weight, both, preferred_element_type=f32)

    def early_half(dest):
        return (x % 2) ^ (dest % 2 != x // 2).astype(jnp.int32)

    def up(value):
        return around(value.astype(bf16), "section", 1)

    def down(value):
        return around(value.astype(bf16), "section", -1)

    put = lambda part, at, line=0: lax.dynamic_update_slice(weight, part[:, None], (line, at % count, 0, 0))
    weight = put(below, x + 3)
    weight = put(above, x + 1)
    dest, weight = lax.optimization_barrier(((position + far) % sections, weight))
    plane = lambda part: lax.dynamic_index_in_dim(part, dest // 2, 0, keepdims=False)
    near = jnp.where(x % 2 == 0, plane(below), plane(above))
    begun = product(jnp.where(dest % 2 == x // 2, plane(held), near)).astype(bf16)
    rising = up(begun)
    beside = jnp.where(x % 2 == 0, plane(above), plane(below))
    across = jnp.where(dest // 2 < LATE, plane(opposite), opposite_rest[0])
    ended = product(jnp.where(dest % 2 == x // 2, beside, across)).astype(bf16)
    falling = down(ended)

    weight = put(tied(opposite, ended), x + 2)
    weight = put(tied(opposite_rest, ended), x + 2, LATE)
    weight = weight.reshape(sections, 2 * shard, depth)

    def block(steps, after=()):
        place = tied(position, *after)
        return lax.dynamic_index_in_dim(weight, (place + steps) % sections, 0, keepdims=False)

    def spread(value, half):
        empty = jnp.zeros_like(value)
        return jnp.concatenate([jnp.where(half == 0, value, empty), jnp.where(half == 0, empty, value)])

    half = early_half((position + far - 1) % sections)
    rising = spread(rising, half)
    half = early_half((position + far + 1) % sections)
    falling = spread(falling, 1 - half)
    def round_of(steps, after):
        upward = product(block(steps, after)) + rising.astype(f32)
        downward = product(block(sections - steps, after)) + falling.astype(f32)
        return upward.astype(bf16), downward.astype(bf16)

    sent = round_of(3, ())
    rising, falling = up(sent[0]), down(sent[1])

    last = sections - 1
    cut = lambda value, s, count=1: value[:, s * width:(s + count) * width]
    arrived = incoming
    given = tied(jnp.where(position == 0, cut(arrived, 2, 2), cut(act, last - 3, 2)), *sent)
    passed = lax.ppermute(given, "section", [(0, 2), (last, last - 2)])
    sent = round_of(2, ())
    rising, falling = up(sent[0]), down(sent[1])

    sent = round_of(1, ())
    rising, falling = up(sent[0]), down(sent[1])

    ends = (position == 0) | (position == last)
    low = position < far
    first = position == 0
    onward = jnp.where(first, cut(arrived, 1), jnp.where(ends, cut(act, last - 1), jnp.where(low, cut(passed, 1), cut(passed, 0))))
    handed = lax.ppermute(
        onward, "section", [(0, 1), (2, 3), (last, last - 1), (last - 2, last - 3)]
    )
    kept = jnp.where(first, cut(arrived, 0), jnp.where(ends, cut(act, last), jnp.where(low, cut(passed, 0), cut(passed, 1))))
    keeps = ends | (position == 2) | (position == last - 2)
    current = jnp.where(position == 0, fresh_batch, incoming)
    wide = current.astype(f32)
    own = tied(jnp.sum(wide * wide, axis=-1), *sent)
    squares = own + around(own, "tensor", 1)
    features = act.shape[-1] * lax.axis_size("tensor")
    scaling = lax.rsqrt(squares[:, None] / features + 1e-06)

    own_term = product(block(0, sent))
    theirs = own_term[:, rows:] + rising[:, rows:].astype(f32) + falling[:, rows:].astype(f32)
    other = around(theirs.astype(bf16), "core", 1)
    section_out = (wide * tied(scaling, theirs) * section_gains).astype(bf16)[None]
    mine = own_term[:, :rows] + rising[:, :rows].astype(f32) + falling[:, :rows].astype(f32)

    vmem = pl.BlockSpec(memory_space=pltpu.VMEM)
    targets, target_error = pl.pallas_call(
        final_kernel,
        in_specs=[pl.BlockSpec(memory_space=pltpu.SMEM)] + [vmem] * 7,
        out_specs=(vmem, vmem),
        out_shape=(
            jax.ShapeDtypeStruct((rows, width), bf16),
            jax.ShapeDtypeStruct(kept.shape, f32),
        ),
    )(jnp.stack([core, keeps]).astype(jnp.int32), mine.astype(bf16), other, old, hot, same, kept, handed)
    return (targets, section_out, target_error)


def solution(mesh):
    fine = Mesh(mesh.devices.reshape(8, 4, 4, 2, 2), AXES)
    in_specs = (
        P(DP, "section"),
        P("section", ("tensor",) + DP),
        P(DP, ("tensor", "section")),
        P("section", DP, "tensor"),
        P(DP, "tensor"),
        P("section", "tensor"),
        P(DP, None),
    )
    out_specs = (
        P(DP, ("tensor", "section")),
        P("section", DP, "tensor"),
        P(DP, ("tensor", "section")),
    )
    return jax.shard_map(
        on_device, mesh=fine, in_specs=in_specs, out_specs=out_specs, check_vma=False
    )
```

```python
import jax
import jax.numpy as jnp
from jax import lax
from jax.experimental import pallas as pl
from jax.experimental.pallas import tpu as pltpu
from jax.sharding import Mesh, PartitionSpec as P

GRID_SIDE = 16
BLOCK_SIDE = 4
PATCHES = 256
AXES = ("section", "zlo", "x", "core", "tensor")
DP = ("zlo", "x", "core")
LATE = 3


def around(value, axis, steps):
    count = lax.axis_size(axis)
    return lax.ppermute(value, axis, [(i, (i + steps) % count) for i in range(count)])


def tied(value, *others):
    return lax.optimization_barrier((value, *others))[0]


def normed(values, images):
    shaped = values.reshape(images, -1, values.shape[-1])
    center = jnp.mean(shaped, axis=1, keepdims=True)
    off = shaped - center
    spread = jnp.mean(jnp.square(off), axis=1, keepdims=True)
    return (off * lax.rsqrt(spread + 1e-05)).reshape(values.shape)


def transpose_kernel(first, second, out):
    rows = first.shape[0]
    out[:, :rows] = first[...].T
    out[:, rows:] = second[...].T


def transposed(first, second):
    rows, depth = first.shape
    return pl.pallas_call(
        transpose_kernel,
        out_shape=jax.ShapeDtypeStruct((depth, 2 * rows), first.dtype),
    )(first, second)


def ready_kernel(blocks, previous, out, hot):
    images = previous.shape[0] // PATCHES
    out[...] = 0.5 * normed(previous[...].astype(jnp.float32), images)
    per_side, size = GRID_SIDE // BLOCK_SIDE, BLOCK_SIDE * BLOCK_SIDE
    within = lax.broadcasted_iota(jnp.int32, (size, PATCHES), 0)
    lane = lax.broadcasted_iota(jnp.int32, (size, PATCHES), 1)
    inside = within // BLOCK_SIDE * GRID_SIDE + within % BLOCK_SIDE
    for k in range(hot.shape[0] // size):
        chosen = blocks[0, k]
        corner = chosen // per_side * BLOCK_SIDE * GRID_SIDE + chosen % per_side * BLOCK_SIDE
        hot[k * size:(k + 1) * size] = jnp.where(lane == inside + corner, 1.0, 0.0).astype(hot.dtype)


def final_kernel(core, keeps, mine, other, old, hot, kept, handed, targets, error):
    images = targets.shape[0] // PATCHES
    shard = mine.shape[0] // 2
    first = core[0] == 0
    pieces = []
    for pair in range(2):
        a, b = (part[pair * shard:(pair + 1) * shard] for part in (mine, other))
        pieces += [jnp.where(first, a, b), jnp.where(first, b, a)]
    ordered = jnp.concatenate(pieces, axis=0).T.astype(jnp.float32)
    made = (0.5 * normed(ordered, images) + old[...]).astype(targets.dtype)
    targets[...] = made
    picked = jnp.dot(hot[...], made[:PATCHES], preferred_element_type=jnp.float32)
    predicted = jnp.where(keeps[0] == 1, kept[...], handed[...])
    error[...] = predicted.astype(jnp.float32) - picked


def on_device(context, out_weight, previous, section_act, fresh_batch, section_gains, mask_blocks):
    f32, bf16 = jnp.float32, jnp.bfloat16
    sections = lax.axis_size("section")
    position, x, core = (lax.axis_index(name) for name in ("section", "x", "core"))
    rows, width = previous.shape
    act = section_act[0]
    depth, shard = out_weight.shape
    far = sections // 2

    held = lax.all_gather(out_weight.T, "zlo", axis=0, tiled=False)
    below = around(held, "x", 1)
    above = around(held, "x", -1)
    incoming = around(act, "section", 1)
    both = transposed(context, around(context, "core", 1))
    count = lax.axis_size("x")
    weight = jnp.broadcast_to(held[:, None], (held.shape[0], count, shard, depth))

    smem, vmem = (pl.BlockSpec(memory_space=space) for space in (pltpu.SMEM, pltpu.VMEM))
    masked = mask_blocks.shape[1] * BLOCK_SIDE * BLOCK_SIDE
    old, hot = pl.pallas_call(
        ready_kernel,
        in_specs=[smem, vmem],
        out_specs=(vmem, vmem),
        out_shape=(
            jax.ShapeDtypeStruct((rows, width), f32),
            jax.ShapeDtypeStruct((masked, PATCHES), bf16),
        ),
        cost_estimate=pl.CostEstimate(flops=0, bytes_accessed=8 << 20, transcendentals=0),
    )(mask_blocks, previous)
    above = tied(above, both, old, weight)
    below, incoming = lax.optimization_barrier((below, incoming))
    opposite = around(above[:LATE], "x", -1)
    opposite_rest = around(below[LATE:], "x", 1)

    def product(weight):
        return jnp.dot(weight, both, preferred_element_type=f32)

    def early_half(dest):
        return (x % 2) ^ (dest % 2 != x // 2).astype(jnp.int32)

    def up(value):
        return around(value.astype(bf16), "section", 1)

    def down(value):
        return around(value.astype(bf16), "section", -1)

    put = lambda part, at, line=0: lax.dynamic_update_slice(weight, part[:, None], (line, at % count, 0, 0))
    weight = put(below, x + 3)
    weight = put(above, x + 1)
    dest, weight = lax.optimization_barrier(((position + far) % sections, weight))
    plane = lambda part: lax.dynamic_index_in_dim(part, dest // 2, 0, keepdims=False)
    near = jnp.where(x % 2 == 0, plane(below), plane(above))
    begun = product(jnp.where(dest % 2 == x // 2, plane(held), near)).astype(bf16)
    rising = up(begun)
    beside = jnp.where(x % 2 == 0, plane(above), plane(below))
    across = jnp.where(dest // 2 < LATE, plane(opposite), opposite_rest[0])
    ended = product(jnp.where(dest % 2 == x // 2, beside, across)).astype(bf16)
    falling = down(ended)

    weight = put(tied(opposite, ended), x + 2)
    weight = put(tied(opposite_rest, ended), x + 2, LATE)
    weight = weight.reshape(sections, 2 * shard, depth)

    def block(steps, after=()):
        place = tied(position, *after)
        return lax.dynamic_index_in_dim(weight, (place + steps) % sections, 0, keepdims=False)

    def spread(value, half):
        empty = jnp.zeros_like(value)
        return jnp.concatenate([jnp.where(half == 0, value, empty), jnp.where(half == 0, empty, value)])

    half = early_half((position + far - 1) % sections)
    rising = spread(rising, half)
    half = early_half((position + far + 1) % sections)
    falling = spread(falling, 1 - half)
    def round_of(steps, after):
        ahead, behind = lax.optimization_barrier((block(steps, after), block(sections - steps, after)))
        upward = product(ahead) + rising.astype(f32)
        downward = product(behind) + falling.astype(f32)
        return upward.astype(bf16), downward.astype(bf16)

    sent = round_of(3, (ended,))
    rising, falling = up(sent[0]), down(sent[1])

    last = sections - 1
    cut = lambda value, s, count=1: value[:, s * width:(s + count) * width]
    arrived = incoming
    given = tied(jnp.where(position == 0, cut(arrived, 2, 2), cut(act, last - 3, 2)), *sent)
    passed = lax.ppermute(given, "section", [(0, 2), (last, last - 2)])
    sent = round_of(2, sent)
    rising, falling = up(sent[0]), down(sent[1])

    sent = round_of(1, sent)
    rising, falling = up(sent[0]), down(sent[1])

    ends = (position == 0) | (position == last)
    low = position < far
    first = position == 0
    onward = jnp.where(first, cut(arrived, 1), jnp.where(ends, cut(act, last - 1), jnp.where(low, cut(passed, 1), cut(passed, 0))))
    handed = lax.ppermute(
        onward, "section", [(0, 1), (2, 3), (last, last - 1), (last - 2, last - 3)]
    )
    kept = jnp.where(first, cut(arrived, 0), jnp.where(ends, cut(act, last), jnp.where(low, cut(passed, 0), cut(passed, 1))))
    keeps = ends | (position == 2) | (position == last - 2)
    current = jnp.where(position == 0, fresh_batch, incoming)
    wide = current.astype(f32)
    own = tied(jnp.sum(wide * wide, axis=-1), *sent)
    squares = own + around(own, "tensor", 1)
    features = act.shape[-1] * lax.axis_size("tensor")
    scaling = lax.rsqrt(squares[:, None] / features + 1e-06)

    own_weight = tied(block(0, sent))
    total = lambda part: jnp.dot(own_weight, both[:, part], preferred_element_type=f32) + (
        rising[:, part].astype(f32) + falling[:, part].astype(f32)
    )
    theirs = total(slice(rows, None))
    other = around(theirs.astype(bf16), "core", 1)
    section_out = (wide * tied(scaling, theirs) * section_gains).astype(bf16)[None]
    mine = total(slice(None, rows))
    targets, target_error = pl.pallas_call(
        final_kernel,
        in_specs=[smem] * 2 + [vmem] * 6,
        out_specs=(vmem, vmem),
        out_shape=(
            jax.ShapeDtypeStruct((rows, width), bf16),
            jax.ShapeDtypeStruct((masked, width), f32),
        ),
    )(core.astype(jnp.int32).reshape(1), keeps.astype(jnp.int32).reshape(1), mine.astype(bf16), other, old, hot, kept, handed)
    return (targets, section_out, target_error)


def solution(mesh):
    fine = Mesh(mesh.devices.reshape(8, 4, 4, 2, 2), AXES)
    in_specs = (
        P(DP, "section"),
        P("section", ("tensor",) + DP),
        P(DP, ("tensor", "section")),
        P("section", DP, "tensor"),
        P(DP, "tensor"),
        P("section", "tensor"),
        P(DP, None),
    )
    out_specs = (
        P(DP, ("tensor", "section")),
        P("section", DP, "tensor"),
        P(DP, ("tensor", "section")),
    )
    return jax.shard_map(
        on_device, mesh=fine, in_specs=in_specs, out_specs=out_specs, check_vma=False
    )
```

```python
import jax
import jax.numpy as jnp
from jax import lax
from jax.experimental import pallas as pl
from jax.experimental.pallas import tpu as pltpu
from jax.sharding import Mesh, PartitionSpec as P

GRID_SIDE = 16
BLOCK_SIDE = 4
PATCHES = 256
AXES = ("section", "zlo", "x", "core", "tensor")
DP = ("zlo", "x", "core")
LATE = 3


def around(value, axis, steps):
    count = lax.axis_size(axis)
    return lax.ppermute(value, axis, [(i, (i + steps) % count) for i in range(count)])


def tied(value, *others):
    return lax.optimization_barrier((value, *others))[0]


def normed(values, images):
    shaped = values.reshape(images, -1, values.shape[-1])
    center = jnp.mean(shaped, axis=1, keepdims=True)
    off = shaped - center
    spread = jnp.mean(jnp.square(off), axis=1, keepdims=True)
    return (off * lax.rsqrt(spread + 1e-05)).reshape(values.shape)


def transpose_kernel(first, second, out):
    rows = first.shape[0]
    out[:, :rows] = first[...].T
    out[:, rows:] = second[...].T


def transposed(first, second):
    rows, depth = first.shape
    return pl.pallas_call(
        transpose_kernel,
        out_shape=jax.ShapeDtypeStruct((depth, 2 * rows), first.dtype),
        compiler_params=pltpu.CompilerParams(vmem_limit_bytes=8 << 20),
    )(first, second)


def whole_kernel(x, held, above, opposite, rest, below, out):
    lines, count = out.shape[:2]
    for z in range(lines):
        across = opposite[z] if z < LATE else rest[z - LATE]
        for steps, part in enumerate((held[z], above[z], across, below[z])):
            out[z, (x[0] + steps) % count] = part


def whole_weight(x, *parts):
    lines, shard, depth = parts[0].shape
    return pl.pallas_call(
        whole_kernel,
        in_specs=[pl.BlockSpec(memory_space=pltpu.SMEM)] + [pl.BlockSpec(memory_space=pltpu.VMEM)] * len(parts),
        out_shape=jax.ShapeDtypeStruct((lines, 4, shard, depth), parts[0].dtype),
        compiler_params=pltpu.CompilerParams(vmem_limit_bytes=8 << 20),
    )(x.astype(jnp.int32).reshape(1), *parts)


def ready_kernel(blocks, previous, out, hot):
    images = previous.shape[0] // PATCHES
    out[...] = 0.5 * normed(previous[...].astype(jnp.float32), images)
    per_side, size = GRID_SIDE // BLOCK_SIDE, BLOCK_SIDE * BLOCK_SIDE
    within = lax.broadcasted_iota(jnp.int32, (size, PATCHES), 0)
    lane = lax.broadcasted_iota(jnp.int32, (size, PATCHES), 1)
    inside = within // BLOCK_SIDE * GRID_SIDE + within % BLOCK_SIDE
    for k in range(hot.shape[0] // size):
        chosen = blocks[0, k]
        corner = chosen // per_side * BLOCK_SIDE * GRID_SIDE + chosen % per_side * BLOCK_SIDE
        hot[k * size:(k + 1) * size] = jnp.where(lane == inside + corner, 1.0, 0.0).astype(hot.dtype)


def final_kernel(core, keeps, mine, other, old, hot, kept, handed, targets, error):
    images = targets.shape[0] // PATCHES
    shard = mine.shape[0] // 2
    first = core[0] == 0
    pieces = []
    for pair in range(2):
        a, b = (part[pair * shard:(pair + 1) * shard] for part in (mine, other))
        pieces += [jnp.where(first, a, b), jnp.where(first, b, a)]
    ordered = jnp.concatenate(pieces, axis=0).T.astype(jnp.float32)
    made = (0.5 * normed(ordered, images) + old[...]).astype(targets.dtype)
    targets[...] = made
    picked = jnp.dot(hot[...], made[:PATCHES], preferred_element_type=jnp.float32)
    predicted = jnp.where(keeps[0] == 1, kept[...], handed[...])
    error[...] = predicted.astype(jnp.float32) - picked


def on_device(context, out_weight, previous, section_act, fresh_batch, section_gains, mask_blocks):
    f32, bf16 = jnp.float32, jnp.bfloat16
    sections = lax.axis_size("section")
    position, x, core = (lax.axis_index(name) for name in ("section", "x", "core"))
    rows, width = previous.shape
    act = section_act[0]
    depth, shard = out_weight.shape
    far = sections // 2

    held = lax.all_gather(out_weight.T, "zlo", axis=0, tiled=False)
    below = around(held, "x", 1)
    above = around(held, "x", -1)
    incoming = around(act, "section", 1)
    both = transposed(context, around(context, "core", 1))

    smem, vmem = (pl.BlockSpec(memory_space=space) for space in (pltpu.SMEM, pltpu.VMEM))
    masked = mask_blocks.shape[1] * BLOCK_SIDE * BLOCK_SIDE
    old, hot = pl.pallas_call(
        ready_kernel,
        in_specs=[smem, vmem],
        out_specs=(vmem, vmem),
        out_shape=(
            jax.ShapeDtypeStruct((rows, width), f32),
            jax.ShapeDtypeStruct((masked, PATCHES), bf16),
        ),
        compiler_params=pltpu.CompilerParams(vmem_limit_bytes=8 << 20),
        cost_estimate=pl.CostEstimate(flops=0, bytes_accessed=8 << 20, transcendentals=0),
    )(mask_blocks, previous)
    above = tied(above, both, old)
    below, incoming = lax.optimization_barrier((below, incoming))
    opposite = around(above[:LATE], "x", -1)
    opposite_rest = around(below[LATE:], "x", 1)

    def product(weight):
        return jnp.dot(weight, both, preferred_element_type=f32)

    def early_half(dest):
        return (x % 2) ^ (dest % 2 != x // 2).astype(jnp.int32)

    def up(value):
        return around(value.astype(bf16), "section", 1)

    def down(value):
        return around(value.astype(bf16), "section", -1)

    dest = (position + far) % sections
    plane = lambda part: lax.dynamic_index_in_dim(part, dest // 2, 0, keepdims=False)
    near = jnp.where(x % 2 == 0, plane(below), plane(above))
    begun = product(jnp.where(dest % 2 == x // 2, plane(held), near)).astype(bf16)
    rising = up(begun)
    beside = jnp.where(x % 2 == 0, plane(above), plane(below))
    across = jnp.where(dest // 2 < LATE, plane(opposite), opposite_rest[0])
    ended = product(jnp.where(dest % 2 == x // 2, beside, across)).astype(bf16)
    falling = down(ended)

    weight = whole_weight(x, held, above, tied(opposite, ended), opposite_rest, below)
    weight = weight.reshape(sections, 2 * shard, depth)

    def block(steps, after=()):
        place = tied(position, *after)
        return lax.dynamic_index_in_dim(weight, (place + steps) % sections, 0, keepdims=False)

    def spread(value, half):
        empty = jnp.zeros_like(value)
        return jnp.concatenate([jnp.where(half == 0, value, empty), jnp.where(half == 0, empty, value)])

    half = early_half((position + far - 1) % sections)
    rising = spread(rising, half)
    half = early_half((position + far + 1) % sections)
    falling = spread(falling, 1 - half)
    def round_of(steps, after):
        upward = product(block(steps, after)) + rising.astype(f32)
        downward = product(block(sections - steps, after)) + falling.astype(f32)
        return upward.astype(bf16), downward.astype(bf16)

    sent = round_of(3, ())
    rising, falling = up(sent[0]), down(sent[1])

    last = sections - 1
    cut = lambda value, s, count=1: value[:, s * width:(s + count) * width]
    arrived = incoming
    given = tied(jnp.where(position == 0, cut(arrived, 2, 2), cut(act, last - 3, 2)), *sent)
    passed = lax.ppermute(given, "section", [(0, 2), (last, last - 2)])
    sent = round_of(2, ())
    rising, falling = up(sent[0]), down(sent[1])

    sent = round_of(1, ())
    rising, falling = up(sent[0]), down(sent[1])

    ends = (position == 0) | (position == last)
    low = position < far
    first = position == 0
    onward = jnp.where(first, cut(arrived, 1), jnp.where(ends, cut(act, last - 1), jnp.where(low, cut(passed, 1), cut(passed, 0))))
    handed = lax.ppermute(
        onward, "section", [(0, 1), (2, 3), (last, last - 1), (last - 2, last - 3)]
    )
    kept = jnp.where(first, cut(arrived, 0), jnp.where(ends, cut(act, last), jnp.where(low, cut(passed, 0), cut(passed, 1))))
    keeps = ends | (position == 2) | (position == last - 2)
    current = jnp.where(position == 0, fresh_batch, incoming)
    wide = current.astype(f32)
    own = tied(jnp.sum(wide * wide, axis=-1), *sent)
    squares = own + around(own, "tensor", 1)
    features = act.shape[-1] * lax.axis_size("tensor")
    scaling = lax.rsqrt(squares[:, None] / features + 1e-06)

    own_weight = block(0)
    total = lambda part: jnp.dot(own_weight, both[:, part], preferred_element_type=f32) + (
        rising[:, part].astype(f32) + falling[:, part].astype(f32)
    )
    theirs = total(slice(rows, None))
    other = around(theirs.astype(bf16), "core", 1)
    section_out = (wide * tied(scaling, theirs) * section_gains).astype(bf16)[None]
    mine = total(slice(None, rows))
    targets, target_error = pl.pallas_call(
        final_kernel,
        in_specs=[smem] * 2 + [vmem] * 6,
        out_specs=(vmem, vmem),
        out_shape=(
            jax.ShapeDtypeStruct((rows, width), bf16),
            jax.ShapeDtypeStruct((masked, width), f32),
        ),
        compiler_params=pltpu.CompilerParams(vmem_limit_bytes=12 << 20),
    )(core.astype(jnp.int32).reshape(1), keeps.astype(jnp.int32).reshape(1), mine.astype(bf16), other, old, hot, kept, handed)
    return (targets, section_out, target_error)


def solution(mesh):
    fine = Mesh(mesh.devices.reshape(8, 4, 4, 2, 2), AXES)
    in_specs = (
        P(DP, "section"),
        P("section", ("tensor",) + DP),
        P(DP, ("tensor", "section")),
        P("section", DP, "tensor"),
        P(DP, "tensor"),
        P("section", "tensor"),
        P(DP, None),
    )
    out_specs = (
        P(DP, ("tensor", "section")),
        P("section", DP, "tensor"),
        P(DP, ("tensor", "section")),
    )
    return jax.shard_map(
        on_device, mesh=fine, in_specs=in_specs, out_specs=out_specs, check_vma=False
    )
```

```python
import jax
import jax.numpy as jnp
from jax import lax
from jax.experimental import pallas as pl
from jax.experimental.pallas import tpu as pltpu
from jax.sharding import Mesh, PartitionSpec as P

GRID_SIDE = 16
BLOCK_SIDE = 4
PATCHES = 256
AXES = ("section", "zlo", "x", "core", "tensor")
DP = ("zlo", "x", "core")
LATE = 3


def around(value, axis, steps):
    count = lax.axis_size(axis)
    return lax.ppermute(value, axis, [(i, (i + steps) % count) for i in range(count)])


def tied(value, *others):
    return lax.optimization_barrier((value, *others))[0]


def normed(values, images):
    shaped = values.reshape(images, -1, values.shape[-1])
    center = jnp.mean(shaped, axis=1, keepdims=True)
    off = shaped - center
    spread = jnp.mean(jnp.square(off), axis=1, keepdims=True)
    return (off * lax.rsqrt(spread + 1e-05)).reshape(values.shape)


def transpose_kernel(first, second, out):
    rows = first.shape[0]
    out[:, :rows] = first[...].T
    out[:, rows:] = second[...].T


def transposed(first, second):
    rows, depth = first.shape
    return pl.pallas_call(
        transpose_kernel,
        out_shape=jax.ShapeDtypeStruct((depth, 2 * rows), first.dtype),
        compiler_params=pltpu.CompilerParams(vmem_limit_bytes=8 << 20),
    )(first, second)


def whole_kernel(x, held, above, opposite, rest, below, out):
    lines, count = out.shape[:2]
    for z in range(lines):
        across = opposite[z] if z < LATE else rest[z - LATE]
        for steps, part in enumerate((held[z], above[z], across, below[z])):
            out[z, (x[0] + steps) % count] = part


def whole_weight(x, *parts):
    lines, shard, depth = parts[0].shape
    return pl.pallas_call(
        whole_kernel,
        in_specs=[pl.BlockSpec(memory_space=pltpu.SMEM)] + [pl.BlockSpec(memory_space=pltpu.VMEM)] * len(parts),
        out_shape=jax.ShapeDtypeStruct((lines, 4, shard, depth), parts[0].dtype),
        compiler_params=pltpu.CompilerParams(vmem_limit_bytes=8 << 20),
    )(x.astype(jnp.int32).reshape(1), *parts)


def ready_kernel(blocks, previous, out, hot):
    images = previous.shape[0] // PATCHES
    out[...] = 0.5 * normed(previous[...].astype(jnp.float32), images)
    per_side, size = GRID_SIDE // BLOCK_SIDE, BLOCK_SIDE * BLOCK_SIDE
    within = lax.broadcasted_iota(jnp.int32, (size, PATCHES), 0)
    lane = lax.broadcasted_iota(jnp.int32, (size, PATCHES), 1)
    inside = within // BLOCK_SIDE * GRID_SIDE + within % BLOCK_SIDE
    for k in range(hot.shape[0] // size):
        chosen = blocks[0, k]
        corner = chosen // per_side * BLOCK_SIDE * GRID_SIDE + chosen % per_side * BLOCK_SIDE
        hot[k * size:(k + 1) * size] = jnp.where(lane == inside + corner, 1.0, 0.0).astype(hot.dtype)


def final_kernel(core, keeps, mine, other, old, hot, kept, handed, targets, error):
    images = targets.shape[0] // PATCHES
    shard = mine.shape[0] // 2
    first = core[0] == 0
    pieces = []
    for pair in range(2):
        a, b = (part[pair * shard:(pair + 1) * shard] for part in (mine, other))
        pieces += [jnp.where(first, a, b), jnp.where(first, b, a)]
    ordered = jnp.concatenate(pieces, axis=0).T.astype(jnp.float32)
    made = (0.5 * normed(ordered, images) + old[...]).astype(targets.dtype)
    targets[...] = made
    picked = jnp.dot(hot[...], made[:PATCHES], preferred_element_type=jnp.float32)
    predicted = jnp.where(keeps[0] == 1, kept[...], handed[...])
    error[...] = predicted.astype(jnp.float32) - picked


def on_device(context, out_weight, previous, section_act, fresh_batch, section_gains, mask_blocks):
    f32, bf16 = jnp.float32, jnp.bfloat16
    sections = lax.axis_size("section")
    position, x, core = (lax.axis_index(name) for name in ("section", "x", "core"))
    rows, width = previous.shape
    act = section_act[0]
    depth, shard = out_weight.shape
    far = sections // 2

    held = lax.all_gather(out_weight.T, "zlo", axis=0, tiled=False)
    below = around(held, "x", 1)
    above = around(held, "x", -1)
    incoming = around(act, "section", 1)
    both = transposed(context, around(context, "core", 1))

    smem, vmem = (pl.BlockSpec(memory_space=space) for space in (pltpu.SMEM, pltpu.VMEM))
    masked = mask_blocks.shape[1] * BLOCK_SIDE * BLOCK_SIDE
    old, hot = pl.pallas_call(
        ready_kernel,
        in_specs=[smem, vmem],
        out_specs=(vmem, vmem),
        out_shape=(
            jax.ShapeDtypeStruct((rows, width), f32),
            jax.ShapeDtypeStruct((masked, PATCHES), bf16),
        ),
        compiler_params=pltpu.CompilerParams(vmem_limit_bytes=8 << 20),
        cost_estimate=pl.CostEstimate(flops=0, bytes_accessed=8 << 20, transcendentals=0),
    )(mask_blocks, previous)
    last = sections - 1
    cut = lambda value, s, count=1: value[:, s * width:(s + count) * width]
    arrived = incoming
    given = jnp.where(position == 0, cut(arrived, 2, 2), cut(act, last - 3, 2))
    passed = lax.ppermute(given, "section", [(0, 2), (last, last - 2)])
    above = tied(above, both, old, given)
    below, incoming = lax.optimization_barrier((below, incoming))
    opposite = around(above[:LATE], "x", -1)
    opposite_rest = around(below[LATE:], "x", 1)

    def product(weight):
        return jnp.dot(weight, both, preferred_element_type=f32)

    def early_half(dest):
        return (x % 2) ^ (dest % 2 != x // 2).astype(jnp.int32)

    def up(value):
        return around(value.astype(bf16), "section", 1)

    def down(value):
        return around(value.astype(bf16), "section", -1)

    dest = tied((position + far) % sections, passed)
    plane = lambda part: lax.dynamic_index_in_dim(part, dest // 2, 0, keepdims=False)
    near = jnp.where(x % 2 == 0, plane(below), plane(above))
    begun = product(jnp.where(dest % 2 == x // 2, plane(held), near)).astype(bf16)
    rising = up(begun)
    beside = jnp.where(x % 2 == 0, plane(above), plane(below))
    across = jnp.where(dest // 2 < LATE, plane(opposite), opposite_rest[0])
    ended = product(jnp.where(dest % 2 == x // 2, beside, across)).astype(bf16)
    falling = down(ended)

    weight = whole_weight(x, held, above, tied(opposite, ended), opposite_rest, below)
    weight = weight.reshape(sections, 2 * shard, depth)

    def block(steps, after=()):
        place = tied(position, *after)
        return lax.dynamic_index_in_dim(weight, (place + steps) % sections, 0, keepdims=False)

    def spread(value, half):
        empty = jnp.zeros_like(value)
        return jnp.concatenate([jnp.where(half == 0, value, empty), jnp.where(half == 0, empty, value)])

    half = early_half((position + far - 1) % sections)
    rising = spread(rising, half)
    half = early_half((position + far + 1) % sections)
    falling = spread(falling, 1 - half)
    def round_of(steps, after):
        upward = product(block(steps, after)) + rising.astype(f32)
        downward = product(block(sections - steps, after)) + falling.astype(f32)
        return upward.astype(bf16), downward.astype(bf16)

    sent = round_of(3, ())
    rising, falling = up(sent[0]), down(sent[1])

    sent = round_of(2, ())
    rising, falling = up(sent[0]), down(sent[1])

    ends = (position == 0) | (position == last)
    low = position < far
    first = position == 0
    onward = jnp.where(first, cut(arrived, 1), jnp.where(ends, cut(act, last - 1), jnp.where(low, cut(passed, 1), cut(passed, 0))))
    handed = lax.ppermute(
        onward, "section", [(0, 1), (2, 3), (last, last - 1), (last - 2, last - 3)]
    )
    kept = jnp.where(first, cut(arrived, 0), jnp.where(ends, cut(act, last), jnp.where(low, cut(passed, 0), cut(passed, 1))))
    keeps = ends | (position == 2) | (position == last - 2)
    sent = round_of(1, (handed,))
    rising, falling = up(sent[0]), down(sent[1])

    current = jnp.where(position == 0, fresh_batch, incoming)
    wide = current.astype(f32)
    own = tied(jnp.sum(wide * wide, axis=-1), *sent)
    squares = own + around(own, "tensor", 1)
    features = act.shape[-1] * lax.axis_size("tensor")
    scaling = lax.rsqrt(squares[:, None] / features + 1e-06)

    own_weight = block(0)
    total = lambda part: jnp.dot(own_weight, both[:, part], preferred_element_type=f32) + (
        rising[:, part].astype(f32) + falling[:, part].astype(f32)
    )
    theirs = total(slice(rows, None))
    other = around(theirs.astype(bf16), "core", 1)
    section_out = (wide * tied(scaling, theirs) * section_gains).astype(bf16)[None]
    mine = total(slice(None, rows))
    targets, target_error = pl.pallas_call(
        final_kernel,
        in_specs=[smem] * 2 + [vmem] * 6,
        out_specs=(vmem, vmem),
        out_shape=(
            jax.ShapeDtypeStruct((rows, width), bf16),
            jax.ShapeDtypeStruct((masked, width), f32),
        ),
        compiler_params=pltpu.CompilerParams(vmem_limit_bytes=12 << 20),
    )(core.astype(jnp.int32).reshape(1), keeps.astype(jnp.int32).reshape(1), mine.astype(bf16), other, old, hot, kept, handed)
    return (targets, section_out, target_error)


def solution(mesh):
    fine = Mesh(mesh.devices.reshape(8, 4, 4, 2, 2), AXES)
    in_specs = (
        P(DP, "section"),
        P("section", ("tensor",) + DP),
        P(DP, ("tensor", "section")),
        P("section", DP, "tensor"),
        P(DP, "tensor"),
        P("section", "tensor"),
        P(DP, None),
    )
    out_specs = (
        P(DP, ("tensor", "section")),
        P("section", DP, "tensor"),
        P(DP, ("tensor", "section")),
    )
    return jax.shard_map(
        on_device, mesh=fine, in_specs=in_specs, out_specs=out_specs, check_vma=False
    )
```

```python
import jax
import jax.numpy as jnp
from jax import lax
from jax.experimental import pallas as pl
from jax.experimental.pallas import tpu as pltpu
from jax.sharding import Mesh, PartitionSpec as P

GRID_SIDE = 16
BLOCK_SIDE = 4
PATCHES = 256
AXES = ("section", "zlo", "x", "core", "tensor")
DP = ("zlo", "x", "core")
LATE = 2


def around(value, axis, steps):
    count = lax.axis_size(axis)
    return lax.ppermute(value, axis, [(i, (i + steps) % count) for i in range(count)])


def tied(value, *others):
    return lax.optimization_barrier((value, *others))[0]


def normed(values, images):
    shaped = values.reshape(images, -1, values.shape[-1])
    center = jnp.mean(shaped, axis=1, keepdims=True)
    off = shaped - center
    spread = jnp.mean(jnp.square(off), axis=1, keepdims=True)
    return (off * lax.rsqrt(spread + 1e-05)).reshape(values.shape)


def transpose_kernel(first, second, out):
    rows = first.shape[0]
    out[:, :rows] = first[...].T
    out[:, rows:] = second[...].T


def transposed(first, second):
    rows, depth = first.shape
    return pl.pallas_call(
        transpose_kernel,
        out_shape=jax.ShapeDtypeStruct((depth, 2 * rows), first.dtype),
        compiler_params=pltpu.CompilerParams(vmem_limit_bytes=8 << 20),
    )(first, second)


def whole_kernel(x, held, above, opposite, rest, below, out):
    lines, count = out.shape[:2]
    for z in range(lines):
        across = opposite[z] if z < LATE else rest[z - LATE]
        for steps, part in enumerate((held[z], above[z], across, below[z])):
            out[z, (x[0] + steps) % count] = part


def whole_weight(x, *parts):
    lines, shard, depth = parts[0].shape
    return pl.pallas_call(
        whole_kernel,
        in_specs=[pl.BlockSpec(memory_space=pltpu.SMEM)] + [pl.BlockSpec(memory_space=pltpu.VMEM)] * len(parts),
        out_shape=jax.ShapeDtypeStruct((lines, 4, shard, depth), parts[0].dtype),
        compiler_params=pltpu.CompilerParams(vmem_limit_bytes=8 << 20),
    )(x.astype(jnp.int32).reshape(1), *parts)


def ready_kernel(blocks, hot):
    per_side, size = GRID_SIDE // BLOCK_SIDE, BLOCK_SIDE * BLOCK_SIDE
    within = lax.broadcasted_iota(jnp.int32, (size, PATCHES), 0)
    lane = lax.broadcasted_iota(jnp.int32, (size, PATCHES), 1)
    inside = within // BLOCK_SIDE * GRID_SIDE + within % BLOCK_SIDE
    for k in range(hot.shape[0] // size):
        chosen = blocks[0, k]
        corner = chosen // per_side * BLOCK_SIDE * GRID_SIDE + chosen % per_side * BLOCK_SIDE
        hot[k * size:(k + 1) * size] = jnp.where(lane == inside + corner, 1.0, 0.0).astype(hot.dtype)


def final_kernel(core, keeps, mine, other, previous, hot, kept, handed, targets, error):
    images = targets.shape[0] // PATCHES
    shard = mine.shape[0] // 2
    first = core[0] == 0
    pieces = []
    for pair in range(2):
        a, b = (part[pair * shard:(pair + 1) * shard] for part in (mine, other))
        pieces += [jnp.where(first, a, b), jnp.where(first, b, a)]
    ordered = jnp.concatenate(pieces, axis=0).T.astype(jnp.float32)
    made = (0.5 * (normed(ordered, images) + normed(previous[...].astype(jnp.float32), images))).astype(targets.dtype)
    targets[...] = made
    picked = jnp.dot(hot[...], made[:PATCHES], preferred_element_type=jnp.float32)
    predicted = jnp.where(keeps[0] == 1, kept[...], handed[...])
    error[...] = predicted.astype(jnp.float32) - picked


def on_device(context, out_weight, previous, section_act, fresh_batch, section_gains, mask_blocks):
    f32, bf16 = jnp.float32, jnp.bfloat16
    sections = lax.axis_size("section")
    position, x, core = (lax.axis_index(name) for name in ("section", "x", "core"))
    rows, width = previous.shape
    act = section_act[0]
    depth, shard = out_weight.shape
    far = sections // 2

    held = lax.all_gather(out_weight.T, "zlo", axis=0, tiled=False)
    below = around(held, "x", 1)
    above = around(held, "x", -1)
    incoming = around(act, "section", 1)
    both = transposed(context, around(context, "core", 1))

    smem, vmem = (pl.BlockSpec(memory_space=space) for space in (pltpu.SMEM, pltpu.VMEM))
    masked = mask_blocks.shape[1] * BLOCK_SIDE * BLOCK_SIDE
    hot = pl.pallas_call(
        ready_kernel,
        in_specs=[smem],
        out_specs=vmem,
        out_shape=jax.ShapeDtypeStruct((masked, PATCHES), bf16),
        compiler_params=pltpu.CompilerParams(vmem_limit_bytes=8 << 20),
        cost_estimate=pl.CostEstimate(flops=0, bytes_accessed=1 << 20, transcendentals=0),
    )(mask_blocks)
    above = tied(above, both, hot)
    below, incoming = lax.optimization_barrier((below, incoming))
    opposite = around(above[:LATE], "x", -1)
    opposite_rest = around(below[LATE:], "x", 1)

    def product(weight):
        return jnp.dot(weight, both, preferred_element_type=f32)

    def early_half(dest):
        return (x % 2) ^ (dest % 2 != x // 2).astype(jnp.int32)

    def up(value):
        return around(value.astype(bf16), "section", 1)

    def down(value):
        return around(value.astype(bf16), "section", -1)

    dest = (position + far) % sections
    plane = lambda part: lax.dynamic_index_in_dim(part, dest // 2, 0, keepdims=False)
    near = jnp.where(x % 2 == 0, plane(below), plane(above))
    begun = product(jnp.where(dest % 2 == x // 2, plane(held), near)).astype(bf16)
    rising = up(begun)
    beside = jnp.where(x % 2 == 0, plane(above), plane(below))
    later = lax.dynamic_index_in_dim(opposite_rest, jnp.maximum(dest // 2 - LATE, 0), 0, keepdims=False)
    across = jnp.where(dest // 2 < LATE, plane(opposite), later)
    ended = product(jnp.where(dest % 2 == x // 2, beside, across)).astype(bf16)
    falling = down(ended)

    weight = whole_weight(x, held, above, tied(opposite, ended), opposite_rest, below)
    weight = weight.reshape(sections, 2 * shard, depth)

    def block(steps, after=()):
        place = tied(position, *after)
        return lax.dynamic_index_in_dim(weight, (place + steps) % sections, 0, keepdims=False)

    def spread(value, half):
        empty = jnp.zeros_like(value)
        return jnp.concatenate([jnp.where(half == 0, value, empty), jnp.where(half == 0, empty, value)])

    half = early_half((position + far - 1) % sections)
    rising = spread(rising, half)
    half = early_half((position + far + 1) % sections)
    falling = spread(falling, 1 - half)
    def round_of(steps, after):
        upward = product(block(steps, after)) + rising.astype(f32)
        downward = product(block(sections - steps, after)) + falling.astype(f32)
        return upward.astype(bf16), downward.astype(bf16)

    sent = round_of(3, ())
    rising, falling = up(sent[0]), down(sent[1])

    last = sections - 1
    cut = lambda value, s, count=1: value[:, s * width:(s + count) * width]
    arrived = incoming
    given = tied(jnp.where(position == 0, cut(arrived, 2, 2), cut(act, last - 3, 2)), *sent)
    passed = lax.ppermute(given, "section", [(0, 2), (last, last - 2)])
    sent = round_of(2, ())
    rising, falling = up(sent[0]), down(sent[1])

    sent = round_of(1, ())
    rising, falling = up(sent[0]), down(sent[1])

    ends = (position == 0) | (position == last)
    low = position < far
    first = position == 0
    onward = jnp.where(first, cut(arrived, 1), jnp.where(ends, cut(act, last - 1), jnp.where(low, cut(passed, 1), cut(passed, 0))))
    handed = lax.ppermute(
        onward, "section", [(0, 1), (2, 3), (last, last - 1), (last - 2, last - 3)]
    )
    kept = jnp.where(first, cut(arrived, 0), jnp.where(ends, cut(act, last), jnp.where(low, cut(passed, 0), cut(passed, 1))))
    keeps = ends | (position == 2) | (position == last - 2)
    current = jnp.where(position == 0, fresh_batch, incoming)
    wide = current.astype(f32)
    own = tied(jnp.sum(wide * wide, axis=-1), *sent)
    squares = own + around(own, "tensor", 1)
    features = act.shape[-1] * lax.axis_size("tensor")
    scaling = lax.rsqrt(squares[:, None] / features + 1e-06)

    own_weight = block(0)
    total = lambda part: jnp.dot(own_weight, both[:, part], preferred_element_type=f32) + (
        rising[:, part].astype(f32) + falling[:, part].astype(f32)
    )
    theirs = total(slice(rows, None))
    other = around(theirs.astype(bf16), "core", 1)
    section_out = (wide * tied(scaling, theirs) * section_gains).astype(bf16)[None]
    mine = total(slice(None, rows))
    targets, target_error = pl.pallas_call(
        final_kernel,
        in_specs=[smem] * 2 + [vmem] * 6,
        out_specs=(vmem, vmem),
        out_shape=(
            jax.ShapeDtypeStruct((rows, width), bf16),
            jax.ShapeDtypeStruct((masked, width), f32),
        ),
        compiler_params=pltpu.CompilerParams(vmem_limit_bytes=12 << 20),
    )(core.astype(jnp.int32).reshape(1), keeps.astype(jnp.int32).reshape(1), mine.astype(bf16), other, previous, hot, kept, handed)
    return (targets, section_out, target_error)


def solution(mesh):
    fine = Mesh(mesh.devices.reshape(8, 4, 4, 2, 2), AXES)
    in_specs = (
        P(DP, "section"),
        P("section", ("tensor",) + DP),
        P(DP, ("tensor", "section")),
        P("section", DP, "tensor"),
        P(DP, "tensor"),
        P("section", "tensor"),
        P(DP, None),
    )
    out_specs = (
        P(DP, ("tensor", "section")),
        P("section", DP, "tensor"),
        P(DP, ("tensor", "section")),
    )
    return jax.shard_map(
        on_device, mesh=fine, in_specs=in_specs, out_specs=out_specs, check_vma=False
    )
```

```python
import jax
import jax.numpy as jnp
from jax import lax
from jax.experimental import pallas as pl
from jax.experimental.pallas import tpu as pltpu
from jax.sharding import Mesh, PartitionSpec as P

GRID_SIDE = 16
BLOCK_SIDE = 4
PATCHES = 256
AXES = ("section", "zlo", "x", "core", "tensor")
DP = ("zlo", "x", "core")
LATE = 3


def around(value, axis, steps):
    count = lax.axis_size(axis)
    return lax.ppermute(value, axis, [(i, (i + steps) % count) for i in range(count)])


def tied(value, *others):
    return lax.optimization_barrier((value, *others))[0]


def normed(values, images):
    shaped = values.reshape(images, -1, values.shape[-1])
    center = jnp.mean(shaped, axis=1, keepdims=True)
    off = shaped - center
    spread = jnp.mean(jnp.square(off), axis=1, keepdims=True)
    return (off * lax.rsqrt(spread + 1e-05)).reshape(values.shape)


def transpose_kernel(first, second, out):
    rows = first.shape[0]
    out[:, :rows] = first[...].T
    out[:, rows:] = second[...].T


def transposed(first, second):
    rows, depth = first.shape
    return pl.pallas_call(
        transpose_kernel,
        out_shape=jax.ShapeDtypeStruct((depth, 2 * rows), first.dtype),
        compiler_params=pltpu.CompilerParams(vmem_limit_bytes=8 << 20),
    )(first, second)


def whole_kernel(x, held, above, opposite, rest, below, out):
    lines, count = out.shape[:2]
    for z in range(lines):
        across = opposite[z] if z < LATE else rest[z - LATE]
        for steps, part in enumerate((held[z], above[z], across, below[z])):
            out[z, (x[0] + steps) % count] = part


def whole_weight(x, *parts):
    lines, shard, depth = parts[0].shape
    return pl.pallas_call(
        whole_kernel,
        in_specs=[pl.BlockSpec(memory_space=pltpu.SMEM)] + [pl.BlockSpec(memory_space=pltpu.VMEM)] * len(parts),
        out_shape=jax.ShapeDtypeStruct((lines, 4, shard, depth), parts[0].dtype),
        compiler_params=pltpu.CompilerParams(vmem_limit_bytes=8 << 20),
    )(x.astype(jnp.int32).reshape(1), *parts)


def ready_kernel(blocks, hot):
    per_side, size = GRID_SIDE // BLOCK_SIDE, BLOCK_SIDE * BLOCK_SIDE
    within = lax.broadcasted_iota(jnp.int32, (size, PATCHES), 0)
    lane = lax.broadcasted_iota(jnp.int32, (size, PATCHES), 1)
    inside = within // BLOCK_SIDE * GRID_SIDE + within % BLOCK_SIDE
    for k in range(hot.shape[0] // size):
        chosen = blocks[0, k]
        corner = chosen // per_side * BLOCK_SIDE * GRID_SIDE + chosen % per_side * BLOCK_SIDE
        hot[k * size:(k + 1) * size] = jnp.where(lane == inside + corner, 1.0, 0.0).astype(hot.dtype)


def final_kernel(core, keeps, mine, other, previous, hot, kept, handed, targets, error):
    images = targets.shape[0] // PATCHES
    shard = mine.shape[0] // 2
    first = core[0] == 0
    pieces = []
    for pair in range(2):
        a, b = (part[pair * shard:(pair + 1) * shard] for part in (mine, other))
        pieces += [jnp.where(first, a, b), jnp.where(first, b, a)]
    ordered = jnp.concatenate(pieces, axis=0).T.astype(jnp.float32)
    made = (0.5 * (normed(ordered, images) + normed(previous[...].astype(jnp.float32), images))).astype(targets.dtype)
    targets[...] = made
    picked = jnp.dot(hot[...], made[:PATCHES], preferred_element_type=jnp.float32)
    predicted = jnp.where(keeps[0] == 1, kept[...], handed[...])
    error[...] = predicted.astype(jnp.float32) - picked


def on_device(context, out_weight, previous, section_act, fresh_batch, section_gains, mask_blocks):
    f32, bf16 = jnp.float32, jnp.bfloat16
    sections = lax.axis_size("section")
    position, x, core = (lax.axis_index(name) for name in ("section", "x", "core"))
    rows, width = previous.shape
    act = section_act[0]
    depth, shard = out_weight.shape
    far = sections // 2

    held = lax.all_gather(out_weight.T, "zlo", axis=0, tiled=False)
    below = around(held, "x", 1)
    above = around(held, "x", -1)
    incoming = around(act, "section", 1)
    both = transposed(context, around(context, "core", 1))

    smem, vmem = (pl.BlockSpec(memory_space=space) for space in (pltpu.SMEM, pltpu.VMEM))
    masked = mask_blocks.shape[1] * BLOCK_SIDE * BLOCK_SIDE
    hot = pl.pallas_call(
        ready_kernel,
        in_specs=[smem],
        out_specs=vmem,
        out_shape=jax.ShapeDtypeStruct((masked, PATCHES), bf16),
        compiler_params=pltpu.CompilerParams(vmem_limit_bytes=8 << 20),
        cost_estimate=pl.CostEstimate(flops=0, bytes_accessed=1 << 20, transcendentals=0),
    )(mask_blocks)
    above = tied(above, both, hot)
    below, incoming = lax.optimization_barrier((below, incoming))
    opposite = around(above[:LATE], "x", -1)
    opposite_rest = around(below[LATE:], "x", 1)

    def product(weight):
        return jnp.dot(weight, both, preferred_element_type=f32)

    def early_half(dest):
        return (x % 2) ^ (dest % 2 != x // 2).astype(jnp.int32)

    def up(value):
        return around(value.astype(bf16), "section", 1)

    def down(value):
        return around(value.astype(bf16), "section", -1)

    dest = (position + far) % sections
    plane = lambda part: lax.dynamic_index_in_dim(part, dest // 2, 0, keepdims=False)
    near = jnp.where(x % 2 == 0, plane(below), plane(above))
    begun = product(jnp.where(dest % 2 == x // 2, plane(held), near)).astype(bf16)
    rising = up(begun)
    beside = jnp.where(x % 2 == 0, plane(above), plane(below))
    across = jnp.where(dest // 2 < LATE, plane(opposite), opposite_rest[0])
    ended = product(jnp.where(dest % 2 == x // 2, beside, across)).astype(bf16)
    falling = down(ended)

    weight = whole_weight(x, held, above, tied(opposite, ended), opposite_rest, below)
    weight = weight.reshape(sections, 2 * shard, depth)

    def block(steps, after=()):
        place = tied(position, *after)
        return lax.dynamic_index_in_dim(weight, (place + steps) % sections, 0, keepdims=False)

    def spread(value, half):
        empty = jnp.zeros_like(value)
        return jnp.concatenate([jnp.where(half == 0, value, empty), jnp.where(half == 0, empty, value)])

    half = early_half((position + far - 1) % sections)
    rising = spread(rising, half)
    half = early_half((position + far + 1) % sections)
    falling = spread(falling, 1 - half)
    def round_of(steps, after):
        upward = product(block(steps, after)) + rising.astype(f32)
        downward = product(block(sections - steps, after)) + falling.astype(f32)
        return upward.astype(bf16), downward.astype(bf16)

    sent = round_of(3, ())
    rising, falling = up(sent[0]), down(sent[1])

    last = sections - 1
    cut = lambda value, s, count=1: value[:, s * width:(s + count) * width]
    arrived = incoming
    given = tied(jnp.where(position == 0, cut(arrived, 2, 2), cut(act, last - 3, 2)), *sent)
    passed = lax.ppermute(given, "section", [(0, 2), (last, last - 2)])
    sent = round_of(2, ())
    rising, falling = up(sent[0]), down(sent[1])

    sent = round_of(1, ())
    rising, falling = up(sent[0]), down(sent[1])

    ends = (position == 0) | (position == last)
    low = position < far
    first = position == 0
    onward = jnp.where(first, cut(arrived, 1), jnp.where(ends, cut(act, last - 1), jnp.where(low, cut(passed, 1), cut(passed, 0))))
    handed = lax.ppermute(
        onward, "section", [(0, 1), (2, 3), (last, last - 1), (last - 2, last - 3)]
    )
    kept = jnp.where(first, cut(arrived, 0), jnp.where(ends, cut(act, last), jnp.where(low, cut(passed, 0), cut(passed, 1))))
    keeps = ends | (position == 2) | (position == last - 2)
    current = jnp.where(position == 0, fresh_batch, incoming)
    wide = current.astype(f32)
    own = tied(jnp.sum(wide * wide, axis=-1), *sent)
    squares = own + around(own, "tensor", 1)
    features = act.shape[-1] * lax.axis_size("tensor")
    scaling = lax.rsqrt(squares[:, None] / features + 1e-06)

    own_weight = block(0)
    total = lambda part: jnp.dot(own_weight, both[:, part], preferred_element_type=f32) + (
        rising[:, part].astype(f32) + falling[:, part].astype(f32)
    )
    theirs = total(slice(rows, None))
    other = around(theirs.astype(bf16), "core", 1)
    section_out = (wide * tied(scaling, theirs) * section_gains).astype(bf16)[None]
    mine = total(slice(None, rows))
    targets, target_error = pl.pallas_call(
        final_kernel,
        in_specs=[smem] * 2 + [vmem] * 6,
        out_specs=(vmem, vmem),
        out_shape=(
            jax.ShapeDtypeStruct((rows, width), bf16),
            jax.ShapeDtypeStruct((masked, width), f32),
        ),
        compiler_params=pltpu.CompilerParams(vmem_limit_bytes=12 << 20),
    )(core.astype(jnp.int32).reshape(1), keeps.astype(jnp.int32).reshape(1), mine.astype(bf16), other, previous, hot, kept, handed)
    return (targets, section_out, target_error)


def solution(mesh):
    fine = Mesh(mesh.devices.reshape(8, 4, 4, 2, 2), AXES)
    in_specs = (
        P(DP, "section"),
        P("section", ("tensor",) + DP),
        P(DP, ("tensor", "section")),
        P("section", DP, "tensor"),
        P(DP, "tensor"),
        P("section", "tensor"),
        P(DP, None),
    )
    out_specs = (
        P(DP, ("tensor", "section")),
        P("section", DP, "tensor"),
        P(DP, ("tensor", "section")),
    )
    return jax.shard_map(
        on_device, mesh=fine, in_specs=in_specs, out_specs=out_specs, check_vma=False
    )
```
